512 devices in a mesh: dp: 4 (over x), pipe: 8 (over z_lo, core), seq: 16 (over z_hi, y).
Axes of the slice: x: 4, y: 8, z: 8 (z_hi: 2, z_lo: 4; z = z_hi * 4 + z_lo), core: 2. Of those that a mesh axis runs over, the one named last changes fastest.
Arguments:
- query_first: bfloat16 [4, 8, 1024, 4096], P('dp', 'pipe', 'seq'), may hold values from -5 to 5
- key_first: bfloat16 [4, 8, 1024, 512], P('dp', 'pipe', 'seq'), may hold values from -5 to 5
- value_first: bfloat16 [4, 8, 1024, 512], P('dp', 'pipe', 'seq'), may hold values from -36 to 36
- query_second: bfloat16 [4, 8, 1024, 4096], P('dp', 'pipe', 'seq'), may hold values from -5 to 5
- key_second: bfloat16 [4, 8, 1024, 512], P('dp', 'pipe', 'seq'), may hold values from -5 to 5
- value_second: bfloat16 [4, 8, 1024, 512], P('dp', 'pipe', 'seq'), may hold values from -36 to 36
- grad_output: bfloat16 [4, 8, 1024, 4096], P('dp', 'pipe', 'seq'), may hold values from -6 to 6
- gain: bfloat16 [8, 4096], P('pipe'), may hold values from 0.5 to 1.5
Outputs:
- next_input: bfloat16 [4, 8, 1024, 4096], P('dp', 'pipe', 'seq')
- grad_query: bfloat16 [4, 8, 1024, 4096], P('dp', 'pipe', 'seq')
- grad_key: bfloat16 [4, 8, 1024, 512], P('dp', 'pipe', 'seq')
- grad_value: bfloat16 [4, 8, 1024, 512], P('dp', 'pipe', 'seq')
- grad_gain: float32 [8, 4096], P('pipe', 'seq')
The draws below stay inside these ranges and needn't reach their ends.
All inputs are finite; a program needn't handle non-finite values.
Results may differ from the reference program's by a relative error of at most 0.012.
The reference program's roundings to bfloat16 on the way count: a program that leaves them out, or rounds other values in their place, can miss the bound.
Values may be sent and summed in bfloat16 or wider, within the bound.
No kernel may reach another device: no remote copies, remote signals or barrier semaphores. Data moves between devices by JAX's collectives and lax.ppermute only.
A program may use at most 64 MiB of HBM per device.

```python
import math
import jax
import jax.numpy as jnp
from jax import lax

SEQ_LEN = 1024
QH = 32
KVH = 4
HD = 128
REPLICAS = 4
SECTIONS = 8


def drawn_pair(key, salt):
    key = jax.random.fold_in(key, salt)
    query_seed, keys_seed = jax.random.split(key, 2)
    query = jnp.clip(jax.random.normal(query_seed, (REPLICAS, SECTIONS, SEQ_LEN, QH, HD), jnp.float32), -4.0, 4.0)
    keys = jnp.clip(jax.random.normal(keys_seed, (REPLICAS, SECTIONS, SEQ_LEN, KVH, HD), jnp.float32), -4.0, 4.0)
    return (query.reshape(REPLICAS, SECTIONS, SEQ_LEN, QH * HD), keys.reshape(REPLICAS, SECTIONS, SEQ_LEN, KVH * HD))


def scaled_values(key):
    base = jnp.clip(jax.random.normal(key, (REPLICAS, SECTIONS, SEQ_LEN, KVH, HD), jnp.float32), -4.0, 4.0)
    scales = 3.0 ** (jnp.arange(KVH, dtype=jnp.float32) / max(KVH - 1, 1))
    return (base * scales[:, None]).reshape(REPLICAS, SECTIONS, SEQ_LEN, KVH * HD)


def draw_query_first(key, part):
    query, keys = drawn_pair(key, 11)
    return query.astype(jnp.bfloat16)


def draw_key_first(key, part):
    query, keys = drawn_pair(key, 11)
    return keys.astype(jnp.bfloat16)


def draw_query_second(key, part):
    query, keys = drawn_pair(key, 12)
    return query.astype(jnp.bfloat16)


def draw_key_second(key, part):
    query, keys = drawn_pair(key, 12)
    return keys.astype(jnp.bfloat16)


def draw_value_first(key, part):
    key = jax.random.fold_in(key, 21)
    return scaled_values(key).astype(jnp.bfloat16)


def draw_value_second(key, part):
    key = jax.random.fold_in(key, 22)
    return scaled_values(key).astype(jnp.bfloat16)


def level_of(own_key, dims, cuts, smallest, largest):
    loudness = 1.0
    for dim, blocks in cuts:
        heights = jax.random.uniform(jax.random.fold_in(jax.random.fold_in(own_key, 6), dim), (blocks,), jnp.float32, smallest / len(cuts), largest / len(cuts))
        loudness = loudness * jnp.repeat(jnp.exp(heights), dims[dim] // blocks).reshape((-1,) + (1,) * (len(dims) - 1 - dim))
    return loudness


def scatter_about(key, extent, width, bound, shards=(), kind=jnp.bfloat16):
    entries = width * jax.random.normal(key, extent, jnp.float32)
    if shards:
        entries = entries * level_of(key, extent, shards, -0.22, 0.18)
    return jnp.clip(entries, -bound, bound).astype(kind)


def setup_inputs(seed: int = 0) -> dict:
    streams_of = jax.random.split(jax.random.key(seed), 9)
    return {
        "query_first": draw_query_first(jax.random.fold_in(streams_of[8], 71), 0),
        "key_first": draw_key_first(jax.random.fold_in(streams_of[8], 71), 0),
        "value_first": draw_value_first(jax.random.fold_in(streams_of[8], 71), 0),
        "query_second": draw_query_second(jax.random.fold_in(streams_of[8], 71), 0),
        "key_second": draw_key_second(jax.random.fold_in(streams_of[8], 71), 0),
        "value_second": draw_value_second(jax.random.fold_in(streams_of[8], 71), 0),
        "grad_output": scatter_about(streams_of[6], (REPLICAS, SECTIONS, SEQ_LEN, QH * HD), 1.0, 6.0, ((0, 4), (1, 8), (2, 16))),
        "gain": jnp.clip(1.0 + 0.1 * jax.random.normal(streams_of[7], (SECTIONS, QH * HD), jnp.float32), 0.5, 1.5).astype(jnp.bfloat16),
    }


epsilon = 1e-05

def rounded(values):
    return lax.optimization_barrier(values.astype(jnp.bfloat16)).astype(jnp.float32)

def expand_heads(keys):
    length = keys.shape[0]
    grouped = keys.astype(jnp.float32).reshape(length, KVH, 1, HD)
    return jnp.broadcast_to(grouped, (length, KVH, QH // KVH, HD)).reshape(length, QH, HD)

def attention_probs(query, keys):
    length = query.shape[0]
    queries = query.astype(jnp.float32).reshape(length, QH, HD)
    scores = jnp.einsum('ihd,jhd->hij', queries, expand_heads(keys)) * (1.0 / math.sqrt(HD))
    positions = jnp.arange(length)
    allowed = positions[None, :] <= positions[:, None]
    scores = jnp.where(allowed[None], scores, -jnp.inf)
    exponent = jnp.exp(scores - lax.optimization_barrier(jnp.max(scores, axis=-1, keepdims=True)))
    return exponent / lax.optimization_barrier(jnp.sum(exponent, axis=-1, keepdims=True))

def attend(query, keys, values):
    length = query.shape[0]
    probs = attention_probs(query, keys)
    result = jnp.einsum('hij,jhd->ihd', rounded(probs), expand_heads(values))
    return result.reshape(length, QH * HD).astype(jnp.bfloat16)

def attend_backward(query, keys, values, output, grad_attn):
    length = query.shape[0]
    probs = attention_probs(query, keys)
    weights = rounded(probs)
    grad_heads = grad_attn.astype(jnp.float32).reshape(length, QH, HD)
    grad_value = jnp.einsum('hij,ihd->jhd', weights, grad_heads)
    grad_value = grad_value.reshape(length, KVH, QH // KVH, HD).sum(axis=2)
    grad_weights = jnp.einsum('ihd,jhd->hij', grad_heads, expand_heads(values))
    row_dots = lax.optimization_barrier(jnp.sum(grad_heads * output.astype(jnp.float32).reshape(length, QH, HD), axis=-1))
    grad_scores = rounded(probs * (grad_weights - row_dots.T[:, :, None]) * (1.0 / math.sqrt(HD)))
    grad_query = jnp.einsum('hij,jhd->ihd', grad_scores, expand_heads(keys))
    queries = query.astype(jnp.float32).reshape(length, QH, HD)
    grad_key = jnp.einsum('hij,ihd->jhd', grad_scores, queries)
    grad_key = grad_key.reshape(length, KVH, QH // KVH, HD).sum(axis=2)
    return (grad_query.reshape(length, QH * HD).astype(jnp.bfloat16), grad_key.reshape(length, KVH * HD).astype(jnp.bfloat16), grad_value.reshape(length, KVH * HD).astype(jnp.bfloat16))

def section_step(inputs):
    first_query, first_keys, first_values, second_query, second_keys, second_values, upstream, gain_row = inputs
    gain_float = gain_row.astype(jnp.float32)
    first_out = attend(first_query, first_keys, first_values).astype(jnp.float32)
    first_inverse = lax.rsqrt(lax.optimization_barrier(jnp.mean(first_out * first_out, axis=-1, keepdims=True)) + epsilon)
    normed = (gain_float * first_out * first_inverse).astype(jnp.bfloat16)
    second_out = attend(second_query, second_keys, second_values)
    activity = second_out.astype(jnp.float32)
    inverse = lax.rsqrt(lax.optimization_barrier(jnp.mean(activity * activity, axis=-1, keepdims=True)) + epsilon)
    upstream_float = upstream.astype(jnp.float32)
    gained = gain_float * upstream_float
    cross_mean = lax.optimization_barrier(jnp.mean(gained * activity, axis=-1, keepdims=True))
    grad_attn = (gained * inverse - activity * inverse ** 3 * cross_mean).astype(jnp.bfloat16)
    grad_gain = lax.optimization_barrier(jnp.sum(upstream_float * activity * inverse, axis=0))
    grad_query, grad_key, grad_value = attend_backward(second_query, second_keys, second_values, second_out, grad_attn)
    return (normed, grad_query, grad_key, grad_value, grad_gain)

def reference(query_first, key_first, value_first, query_second, key_second, value_second, grad_output, gain):
    replicas = query_first.shape[0]
    sections = query_first.shape[1]
    upstream = jnp.roll(grad_output, -1, axis=1)
    gains = jnp.broadcast_to(gain[None], (replicas,) + gain.shape)

    def flatten(array):
        return array.reshape((replicas * sections,) + array.shape[2:])

    def unflatten(array):
        return array.reshape((replicas, sections) + array.shape[1:])
    inputs = tuple((flatten(array) for array in (query_first, key_first, value_first, query_second, key_second, value_second, upstream, gains)))
    results = lax.map(section_step, inputs)
    normed, grad_query, grad_key, grad_value, grad_gain = [unflatten(array) for array in results]
    return (jnp.roll(normed, 1, axis=1), grad_query, grad_key, grad_value, lax.optimization_barrier(jnp.sum(grad_gain, axis=0)))
```

```python
import functools
import math

import jax
import jax.numpy as jnp
from jax import lax
from jax.experimental import pallas as pl
from jax.experimental.pallas import tpu as pltpu
from jax.sharding import Mesh
from jax.sharding import PartitionSpec as P

HD = 128
EPSILON = 1e-05
SCALE = 1.0 / math.sqrt(HD)
F32 = jnp.float32
BF16 = jnp.bfloat16

NEAR = ((0, 1), (2, 3))
FAR = ((0, 2), (1, 3))
CROSS = ((1, 2), (0, 3))
GROUP = ("zhi", "yhi")
SEQ = ("zhi", "yhi", "ylo")

VMEM = pl.BlockSpec(memory_space=pltpu.VMEM)
SMEM = pl.BlockSpec(memory_space=pltpu.SMEM)


def call(body, outs, inputs, scratch=(), flops=0, moved=0, name=None):
    return pl.pallas_call(
        body,
        out_shape=outs,
        in_specs=[SMEM] + [VMEM] * (len(inputs) - 1),
        out_specs=jax.tree.map(lambda _: VMEM, outs),
        scratch_shapes=list(scratch),
        compiler_params=pltpu.CompilerParams(vmem_limit_bytes=48 * 1024 * 1024),
        cost_estimate=pl.CostEstimate(
            flops=flops, bytes_accessed=moved, transcendentals=0
        ),
        name=name,
    )(*inputs)


def dot_nt(a, b):
    return lax.dot_general(a, b, (((1,), (1,)), ((), ())), preferred_element_type=F32)


def dot_nn(a, b):
    return lax.dot_general(a, b, (((1,), (0,)), ((), ())), preferred_element_type=F32)


def column(row):
    return jnp.broadcast_to(row, (HD, row.shape[1])).T


def row_of(block):
    return jnp.sum(block.T, axis=0, keepdims=True)


def from_place(index, step, count):
    return lax.rem(index - step + count, count)


def biases(where):
    group = where[0]
    odd = lax.rem(group, 2) == 1
    late = group >= 2
    near = jnp.where(odd, 0.0, -jnp.inf).astype(F32)
    far = jnp.where(late, 0.0, -jnp.inf).astype(F32)
    return near, far, far


def masked_scores(keys, queries, bias, n):
    scores = dot_nt(keys, queries) * SCALE
    key_ids = lax.broadcasted_iota(jnp.int32, (n, n), 0)
    query_ids = lax.broadcasted_iota(jnp.int32, (n, n), 1)
    parts = [jnp.where(key_ids <= query_ids, scores[:n], -jnp.inf)]
    for i in range(3):
        parts.append(scores[(i + 1) * n : (i + 2) * n] + bias[i])
    return jnp.concatenate(parts, axis=0)


def forward_head(keys, values_t, queries, bias, n):
    scores = masked_scores(keys, queries, bias, n)
    highest = jnp.max(scores, axis=0, keepdims=True)
    exponent = jnp.exp(scores - highest)
    total = jnp.sum(exponent, axis=0, keepdims=True)
    weights = (exponent * (1.0 / total)).astype(BF16)
    out = dot_nn(values_t, weights).T.astype(BF16)
    return out, highest + jnp.log(total)


def load_keys(kv_refs, at, k_ref, n):
    for i, ref in enumerate(kv_refs):
        k_ref[i * n : (i + 1) * n, :] = ref[:, at : at + HD]


def load_values_t(kv_refs, at, vt_ref, n):
    for i, ref in enumerate(kv_refs):
        vt_ref[:, i * n : (i + 1) * n] = ref[:, at : at + HD].T


def forward_first_body(heads, n, where, q, kv0, kv1, kv2, kv3, out, stats, k_s, vt_s):
    kvs = (kv0, kv1, kv2, kv3)
    load_keys(kvs, 2 * HD, k_s, n)
    load_values_t(kvs, 3 * HD, vt_s, n)
    bias = biases(where)
    square = jnp.zeros((n, HD), F32)
    for h in range(heads):
        cols = slice(h * HD, (h + 1) * HD)
        result, _ = forward_head(k_s[...], vt_s[...], q[:, cols], bias, n)
        out[:, cols] = result
        result = result.astype(F32)
        square = square + result * result
    row = row_of(square)
    for copy in range(stats.shape[0]):
        stats[copy] = jnp.broadcast_to(row, stats.shape[1:])


def assemble(where, pieces, up_s):
    rows = pieces[0].shape[0]
    for k, piece in enumerate(pieces):
        at = pl.multiple_of(from_place(where[1], k, len(pieces)) * rows, rows)
        up_s[pl.ds(at, rows), :] = piece[...]


def forward_second_body(
    heads, n, where, q, kv0, kv1, kv2, kv3, up0, up1, up2, up3, gain, out, lse, stats, k_s, vt_s, up_s
):
    kvs = (kv0, kv1, kv2, kv3)
    assemble(where, (up0, up1, up2, up3), up_s)
    load_keys(kvs, 0, k_s, n)
    load_values_t(kvs, HD, vt_s, n)
    bias = biases(where)
    square = jnp.zeros((n, HD), F32)
    cross = jnp.zeros((n, HD), F32)
    for h in range(heads):
        cols = slice(h * HD, (h + 1) * HD)
        result, logs = forward_head(k_s[...], vt_s[...], q[:, cols], bias, n)
        out[:, cols] = result
        lse[h : h + 1, :] = logs
        result = result.astype(F32)
        square = square + result * result
        cross = cross + gain[:, cols].astype(F32) * up_s[:, cols].astype(F32) * result
    rows = jnp.concatenate(
        [row_of(square), row_of(cross), jnp.zeros((stats.shape[1] - 2, n), F32)], axis=0
    )
    for copy in range(stats.shape[0]):
        stats[copy] = rows


def normed_body(heads, width, where, act, stats, gain, o0, o1, o2, o3):
    outs = (o0, o1, o2, o3)
    rows = o0.shape[0]
    total = stats[0, 0:1] + stats[1, 0:1] + stats[2, 0:1] + stats[3, 0:1]
    inverse = column(lax.rsqrt(total / width + EPSILON))
    inverse = jnp.concatenate([inverse] * heads, axis=1)
    normed = (gain[...].astype(F32) * act[...].astype(F32) * inverse).astype(BF16)
    full = normed
    for k in range(4):
        wanted = lax.rem(where[1] + k, 4)
        for block in range(4):

            @pl.when(wanted == block)
            def _(block=block, k=k):
                outs[k][...] = full[block * rows : (block + 1) * rows]


def gain_body(heads, width, where, act, stats, up0, up1, up2, up3, out, up_s):
    assemble(where, (up0, up1, up2, up3), up_s)
    total = stats[0, 0:1] + stats[1, 0:1] + stats[2, 0:1] + stats[3, 0:1]
    inverse = column(lax.rsqrt(total / width + EPSILON))
    for h in range(heads):
        cols = slice(h * HD, (h + 1) * HD)
        product = up_s[:, cols].astype(F32) * act[:, cols].astype(F32) * inverse
        out[h : h + 1, :] = jnp.sum(product, axis=0, keepdims=True)


def backward_body(
    heads, n, width, where, q, kv0, kv1, kv2, kv3, up0, up1, up2, up3, gain, act, lse, stats,
    dq, dkv0, dkv1, dkv2, dkv3, k_s, kt_s, v_s, up_s, dk_s, dv_s,
):
    kvs = (kv0, kv1, kv2, kv3)
    assemble(where, (up0, up1, up2, up3), up_s)
    load_keys(kvs, 0, k_s, n)
    load_values_t(kvs, 0, kt_s, n)
    load_keys(kvs, HD, v_s, n)
    bias = biases(where)
    totals = stats[0] + stats[1] + stats[2] + stats[3]
    inverse_row = lax.rsqrt(totals[0:1] / width + EPSILON)
    inverse = column(inverse_row)
    shrink = column(inverse_row * inverse_row * inverse_row * (totals[1:2] / width))
    for h in range(heads):
        cols = slice(h * HD, (h + 1) * HD)
        queries = q[:, cols]
        act_h = act[:, cols].astype(F32)
        gained = gain[:, cols].astype(F32) * up_s[:, cols].astype(F32)
        grad = (gained * inverse - act_h * shrink).astype(BF16)
        dots = row_of(grad.astype(F32) * act_h)
        scores = masked_scores(k_s[...], queries, bias, n)
        probs = jnp.exp(scores - lse[h : h + 1, :])
        grad_weights = dot_nt(v_s[...], grad)
        grad_scores = (probs * (grad_weights - dots) * SCALE).astype(BF16)
        dv = dot_nn(probs.astype(BF16), grad)
        dk = dot_nn(grad_scores, queries)
        if h == 0:
            dv_s[...] = dv
            dk_s[...] = dk
        else:
            dv_s[...] += dv
            dk_s[...] += dk
        dq[:, cols] = dot_nn(kt_s[...], grad_scores).T.astype(BF16)
    for i, ref in enumerate((dkv0, dkv1, dkv2, dkv3)):
        ref[:, :HD] = dk_s[i * n : (i + 1) * n].astype(ref.dtype)
        ref[:, HD:] = dv_s[i * n : (i + 1) * n].astype(ref.dtype)


def split_body(where, full, o0, o1, o2, o3):
    width = o0.shape[1]
    for k, out in enumerate((o0, o1, o2, o3)):
        at = pl.multiple_of(lax.rem(where[1] + k, 4) * width, width)
        out[...] = full[:, pl.ds(at, width)]


def join_body(where, p0, p1, p2, p3, out):
    width = p0.shape[1]
    for k, piece in enumerate((p0, p1, p2, p3)):
        at = pl.multiple_of(from_place(where[1], k, 4) * width, width)
        out[:, pl.ds(at, width)] = piece[...]


def sds(shape, dtype):
    return jax.ShapeDtypeStruct(shape, dtype)


def swap_lo(packed):
    return lax.all_to_all(packed, "ylo", split_axis=0, concat_axis=0, tiled=True)


def local(
    query_first, key_first, value_first, query_second, key_second, value_second, grad_output, gain
):
    lo = lax.axis_size("ylo")
    tokens, width = query_first.shape[2:]
    n = tokens * lo
    cols = width // lo
    heads = cols // HD
    pipes = lax.axis_size("pipe")
    ylo = lax.axis_index("ylo")
    group = lax.axis_index(GROUP)
    where = jnp.stack([group, ylo]).astype(jnp.int32)
    gain_cols = lax.dynamic_slice_in_dim(gain, ylo * cols, cols, 1)

    def shifted(pieces, steps):
        got = []
        for k, piece in enumerate(pieces):
            pairs = [
                (p * lo + y, ((p + steps) % pipes) * lo + (y + k) % lo)
                for p in range(pipes)
                for y in range(lo)
            ]
            got.append(lax.ppermute(piece, ("pipe", "ylo"), pairs))
        return got

    kv = jnp.concatenate(
        [
            x[0, 0].reshape(tokens, lo, HD)
            for x in (key_second, value_second, key_first, value_first)
        ],
        axis=2,
    ).transpose(1, 0, 2)
    kv0 = swap_lo(kv).reshape(n, 4 * HD)
    kvs = [kv0] + [lax.ppermute(kv0, GROUP, pairs) for pairs in (NEAR, FAR, CROSS)]

    pieces = call(
        split_body, (sds((tokens, cols), BF16),) * 4, (where, grad_output[0, 0]), name="split"
    )
    up = shifted(pieces, -1)

    def by_heads(query):
        packed = query[0, 0].reshape(tokens, lo, cols).transpose(1, 0, 2)
        return swap_lo(packed).reshape(n, cols)

    q2 = by_heads(query_second)
    q1 = by_heads(query_first)
    keys_shape = (4 * n, HD)
    turned = (HD, 4 * n)
    unit = 2 * 4 * n * n * HD * heads

    out2, lse, stats2 = call(
        functools.partial(forward_second_body, heads, n),
        (sds((n, cols), BF16), sds((heads, n), F32), sds((lo, 8, n), F32)),
        (where, q2, *kvs, *up, gain_cols),
        [pltpu.VMEM(keys_shape, BF16), pltpu.VMEM(turned, BF16), pltpu.VMEM((n, cols), BF16)],
        flops=2 * unit,
        moved=4 << 20,
        name="forward_second",
    )
    stats2 = swap_lo(stats2)
    out1, stats1 = call(
        functools.partial(forward_first_body, heads, n),
        (sds((n, cols), BF16), sds((lo, 8, n), F32)),
        (where, q1, *kvs),
        [pltpu.VMEM(keys_shape, BF16), pltpu.VMEM(turned, BF16)],
        flops=2 * unit,
        moved=4 << 20,
        name="forward_first",
    )
    stats1 = swap_lo(stats1)

    gain_part = call(
        functools.partial(gain_body, heads, width),
        sds((heads, HD), F32),
        (where, out2, stats2, *up),
        [pltpu.VMEM((n, cols), BF16)],
        name="gain_rows",
    )
    replicas = lax.axis_size("dp")
    spread = jnp.broadcast_to(
        gain_part.reshape(1, 4, heads // 4, HD), (replicas, 4, heads // 4, HD)
    ).reshape(replicas * 4, heads // 4, HD)
    shares = lax.all_to_all(spread, ("dp",) + GROUP, split_axis=0, concat_axis=0, tiled=True)
    share = jnp.sum(shares, axis=0)
    turn = [(g * lo + y, y * lo + g) for g in range(4) for y in range(lo)]
    grad_gain = lax.ppermute(share, SEQ, turn).reshape(1, cols // 4)

    dq, dkv0, dkv1, dkv2, dkv3 = call(
        functools.partial(backward_body, heads, n, width),
        (sds((n, cols), BF16), sds((n, 2 * HD), F32)) + (sds((n, 2 * HD), BF16),) * 3,
        (where, q2, *kvs, *up, gain_cols, out2, lse, stats2),
        [
            pltpu.VMEM(keys_shape, BF16),
            pltpu.VMEM(turned, BF16),
            pltpu.VMEM(keys_shape, BF16),
            pltpu.VMEM((n, cols), BF16),
            pltpu.VMEM(keys_shape, F32),
            pltpu.VMEM(keys_shape, F32),
        ],
        flops=5 * unit,
        moved=6 << 20,
        name="backward",
    )
    back = [
        lax.ppermute(part, GROUP, [(b, a) for a, b in pairs])
        for part, pairs in ((dkv1, NEAR), (dkv2, FAR), (dkv3, CROSS))
    ]
    dkv = dkv0 + (back[0].astype(F32) + back[1].astype(F32) + back[2].astype(F32))
    dq = swap_lo(dq.reshape(lo, tokens, cols))
    grad_query = dq.transpose(1, 0, 2).reshape(tokens, width)
    dkv = swap_lo(dkv.astype(BF16).reshape(lo, tokens, 2 * HD))
    grad_key = dkv[:, :, :HD].transpose(1, 0, 2).reshape(tokens, lo * HD)
    grad_value = dkv[:, :, HD:].transpose(1, 0, 2).reshape(tokens, lo * HD)

    normed = call(
        functools.partial(normed_body, heads, width),
        (sds((tokens, cols), BF16),) * 4,
        (where, out1, stats1, gain_cols),
        name="normed",
    )
    arrived = shifted(normed, 1)
    next_input = call(
        join_body, sds((tokens, width), BF16), (where, *arrived), name="join"
    )
    return (
        next_input[None, None],
        grad_query[None, None],
        grad_key[None, None],
        grad_value[None, None],
        grad_gain,
    )


def solution(mesh):
    shape = mesh.devices.shape
    fine = Mesh(
        mesh.devices.reshape(shape[0], shape[1], 2, 2, shape[2] // 4),
        ("dp", "pipe", "zhi", "yhi", "ylo"),
    )
    big = P("dp", "pipe", SEQ, None)
    return jax.shard_map(
        local,
        mesh=fine,
        in_specs=(big,) * 7 + (P("pipe", None),),
        out_specs=(big,) * 4 + (P("pipe", SEQ),),
        check_vma=False,
    )
```

```python
import functools
import math

import jax
import jax.numpy as jnp
from jax import lax
from jax.experimental import pallas as pl
from jax.experimental.pallas import tpu as pltpu
from jax.sharding import Mesh
from jax.sharding import PartitionSpec as P

HD = 128
EPSILON = 1e-05
SCALE = 1.0 / math.sqrt(HD)
F32 = jnp.float32
BF16 = jnp.bfloat16

ROW = ("yhi", "ylo")
SEQ = ("zhi", "yhi", "ylo")
FOUR = 4

VMEM = pl.BlockSpec(memory_space=pltpu.VMEM)
SMEM = pl.BlockSpec(memory_space=pltpu.SMEM)


def call(body, outs, inputs, scratch=(), micros=1.0, name=None):
    return pl.pallas_call(
        body,
        out_shape=outs,
        in_specs=[SMEM] + [VMEM] * (len(inputs) - 1),
        out_specs=jax.tree.map(lambda _: VMEM, outs),
        scratch_shapes=list(scratch),
        compiler_params=pltpu.CompilerParams(vmem_limit_bytes=48 * 1024 * 1024),
        cost_estimate=pl.CostEstimate(
            flops=int(micros * 1e9), bytes_accessed=0, transcendentals=0
        ),
        name=name,
    )(*inputs)


def sds(shape, dtype):
    return jax.ShapeDtypeStruct(shape, dtype)


def dot_nt(a, b):
    return lax.dot_general(a, b, (((1,), (1,)), ((), ())), preferred_element_type=F32)


def dot_nn(a, b):
    return lax.dot_general(a, b, (((1,), (0,)), ((), ())), preferred_element_type=F32)


def column(row):
    return jnp.broadcast_to(row, (HD, row.shape[1])).T


def row_of(block):
    return jnp.sum(block.T, axis=0, keepdims=True)


def attend(keys, values_t, bias, queries):
    scores = dot_nt(keys, queries) + bias[...]
    highest = jnp.max(scores, axis=0, keepdims=True)
    exponent = jnp.exp((scores - highest) * SCALE)
    total = jnp.sum(exponent, axis=0, keepdims=True)
    out = dot_nn(values_t, exponent.astype(BF16)) * (1.0 / total)
    return out.T.astype(BF16), highest * SCALE + jnp.log(total)


def set_bias(where, bias):
    shape = bias.shape
    ahead = lax.broadcasted_iota(jnp.int32, shape, 0) - lax.broadcasted_iota(jnp.int32, shape, 1)
    bias[...] = jnp.where(ahead <= where[0] * shape[1], 0.0, -jnp.inf).astype(F32)


def assemble(where, pieces, full):
    rows = pieces[0].shape[0]
    for k, piece in enumerate(pieces):
        at = pl.multiple_of(lax.rem(where[2] - k + FOUR, FOUR) * rows, rows)
        full[pl.ds(at, rows), :] = piece[...]


def open_body(where, query, keys, values, kv, q0, q1, q2, q3):
    for s in range(kv.shape[0]):
        cols = slice((s % FOUR) * HD, (s % FOUR + 1) * HD)
        kv[s, :, :HD] = keys[:, cols]
        kv[s, :, HD:] = values[:, cols]
    width = q0.shape[1]
    for k, out in enumerate((q0, q1, q2, q3)):
        at = pl.multiple_of(lax.rem(where[2] + k, FOUR) * width, width)
        out[...] = query[:, pl.ds(at, width)]


def pack_body(where, full, out):
    width = out.shape[2]
    for place in range(FOUR):
        out[place] = full[:, place * width : (place + 1) * width]


def join_body(where, p0, p1, p2, p3, out):
    width = p0.shape[1]
    for k, piece in enumerate((p0, p1, p2, p3)):
        at = pl.multiple_of(lax.rem(where[2] - k + FOUR, FOUR) * width, width)
        out[:, pl.ds(at, width)] = piece[...]


def gather_body(where, parts, keys, values, share):
    tokens = keys.shape[0]
    for h in range(FOUR):
        cols = slice(h * HD, (h + 1) * HD)
        total = parts[h, :tokens].astype(F32)
        for s in range(h + FOUR, parts.shape[0], FOUR):
            total = total + parts[s, :tokens].astype(F32)
        keys[:, cols] = total[:, :HD].astype(BF16)
        values[:, cols] = total[:, HD:].astype(BF16)
    terms = parts[0, tokens:].astype(F32)
    for s in range(1, parts.shape[0]):
        terms = terms + parts[s, tokens:].astype(F32)
    share[...] = terms[0:1] + terms[1:2] + terms[2:3]


def forward_body(heads, where, q0, q1, q2, q3, kv, out, lse, q_s, vt_s, bias):
    assemble(where, (q0, q1, q2, q3), q_s)
    set_bias(where, bias)
    vt_s[...] = kv[:, HD:].T
    for h in range(heads):
        cols = slice(h * HD, (h + 1) * HD)
        out[:, cols], lse[h : h + 1, :] = attend(kv[:, :HD], vt_s[...], bias, q_s[:, cols])


def stats_body(heads, where, act, up, gain, stats):
    n = act.shape[0]
    square = jnp.zeros((n, HD), F32)
    cross = jnp.zeros((n, HD), F32)
    for h in range(heads):
        cols = slice(h * HD, (h + 1) * HD)
        value = act[:, cols].astype(F32)
        square = square + value * value
        cross = cross + gain[:, cols].astype(F32) * up[:, cols].astype(F32) * value
    rows = jnp.concatenate(
        [row_of(square), row_of(cross), jnp.zeros((stats.shape[1] - 2, n), F32)], axis=0
    )
    for place in range(FOUR):
        stats[place] = rows


def backward_body(
    heads, width, where, q0, q1, q2, q3, kv, up, gain, act, lse, stats,
    dq0, dq1, dq2, dq3, dkv, q_s, kt_s, bias, dk_s, dv_s, dq_s,
):
    assemble(where, (q0, q1, q2, q3), q_s)
    set_bias(where, bias)
    kt_s[...] = kv[:, :HD].T
    totals = (stats[0] + stats[1]) + (stats[2] + stats[3])
    inverse_row = lax.rsqrt(totals[0:1] / width + EPSILON)
    inverse = column(inverse_row)
    shrink = column(inverse_row * inverse_row * inverse_row * (totals[1:2] / width))
    sums = []
    for h in range(heads):
        cols = slice(h * HD, (h + 1) * HD)
        queries = q_s[:, cols]
        act_h = act[:, cols].astype(F32)
        upstream = up[:, cols].astype(F32)
        sums.append(jnp.sum(upstream * act_h * inverse, axis=0, keepdims=True))
        grad = (gain[:, cols].astype(F32) * upstream * inverse - act_h * shrink).astype(BF16)
        dots = row_of(grad.astype(F32) * act_h)
        scores = dot_nt(kv[:, :HD], queries) * SCALE + bias[...]
        probs = jnp.exp(scores - lse[h : h + 1, :])
        grad_weights = dot_nt(kv[:, HD:], grad)
        grad_scores = (probs * (grad_weights - dots) * SCALE).astype(BF16)
        dv = dot_nn(probs.astype(BF16), grad)
        dk = dot_nn(grad_scores, queries)
        if h == 0:
            dv_s[...] = dv
            dk_s[...] = dk
        else:
            dv_s[...] += dv
            dk_s[...] += dk
        dq_s[:, cols] = dot_nn(kt_s[...], grad_scores).T.astype(BF16)
    tokens = dq0.shape[0]
    for k, out in enumerate((dq0, dq1, dq2, dq3)):
        at = pl.multiple_of(lax.rem(where[2] + k, FOUR) * tokens, tokens)
        out[...] = dq_s[pl.ds(at, tokens), :]
    per = heads // FOUR
    extra = dkv.shape[1] - tokens
    for s in range(dkv.shape[0]):
        rows = slice(s * tokens, (s + 1) * tokens)
        dkv[s, :tokens, :HD] = dk_s[rows].astype(BF16)
        dkv[s, :tokens, HD:] = dv_s[rows].astype(BF16)
        j = s % FOUR
        value = jnp.concatenate(sums[j * per : (j + 1) * per], axis=1)
        value = jnp.where(where[2] == s // FOUR, value, 0.0)
        terms = []
        for _ in range(3):
            term = value.astype(BF16).astype(F32)
            terms.append(term)
            value = value - term
        terms.append(jnp.zeros((extra - 3, value.shape[1]), F32))
        dkv[s, tokens:] = jnp.concatenate(terms, axis=0).astype(BF16)


def first_body(where, q, kv, gain, out, k_s, vt_s, q_s, o_s, bias):
    tokens, width = q.shape
    length = kv.shape[0]
    kv_heads = kv.shape[1] // (2 * HD)
    heads = width // HD
    n = bias.shape[1]
    together = n // tokens
    ids = lax.broadcasted_iota(jnp.int32, (length, n), 0)
    query_ids = lax.broadcasted_iota(jnp.int32, (length, n), 1) % tokens
    block = ids // tokens
    half = (block % 2 + where[1]) % 2
    key_at = half * (length // 2) + (block // 2) * tokens + ids % tokens
    query_at = where[1] * (length // 2) + where[3] * tokens + query_ids
    bias[...] = jnp.where(key_at <= query_at, 0.0, -jnp.inf).astype(F32)
    square = jnp.zeros((tokens, HD), F32)
    for g in range(kv_heads):
        k_s[...] = kv[:, g * HD : (g + 1) * HD]
        vt_s[...] = kv[:, (kv_heads + g) * HD : (kv_heads + g + 1) * HD].T
        for part in range(heads // kv_heads // together):
            start = g * (heads // kv_heads) + part * together
            for i in range(together):
                q_s[i * tokens : (i + 1) * tokens, :] = q[:, (start + i) * HD : (start + i + 1) * HD]
            result, _ = attend(k_s[...], vt_s[...], bias, q_s[...])
            for i in range(together):
                piece = result[i * tokens : (i + 1) * tokens]
                o_s[:, (start + i) * HD : (start + i + 1) * HD] = piece
                piece = piece.astype(F32)
                square = square + piece * piece
    mean = jnp.sum(square, axis=1, keepdims=True) / width
    inverse = jnp.broadcast_to(lax.rsqrt(mean + EPSILON), (tokens, HD))
    for h in range(heads):
        cols = slice(h * HD, (h + 1) * HD)
        out[:, cols] = (gain[:, cols].astype(F32) * o_s[:, cols].astype(F32) * inverse).astype(BF16)


def local(
    query_first, key_first, value_first, query_second, key_second, value_second, grad_output, gain
):
    tokens, width = query_first.shape[2:]
    kv_width = key_first.shape[3]
    n = tokens * FOUR
    cols = width // FOUR
    heads = cols // HD
    places = lax.axis_size(SEQ)
    length = tokens * places
    pipes = lax.axis_size("pipe")
    zhi, yhi, ylo = (lax.axis_index(axis) for axis in SEQ)
    where = jnp.stack([zhi * 2 + yhi, zhi, ylo, yhi * FOUR + ylo]).astype(jnp.int32)
    gain_cols = lax.dynamic_slice_in_dim(gain, ylo * cols, cols, 1)

    def swap(packed, axes):
        return lax.all_to_all(packed, axes, split_axis=0, concat_axis=0, tiled=True)

    def along(value, axis, step, count):
        return lax.ppermute(value, axis, [(i, (i + step) % count) for i in range(count)])

    def ahead(pieces):
        return [pieces[0]] + [along(pieces[k], "ylo", k, FOUR) for k in range(1, FOUR)]

    piece = sds((tokens, cols), BF16)
    kv1 = jnp.concatenate([key_first[0, 0], value_first[0, 0]], axis=1)
    other = lax.ppermute(kv1, "zhi", [(0, 1)])
    up_raw = along(grad_output[0, 0], "pipe", -1, pipes)
    packed, *q2 = call(
        open_body,
        (sds((places, tokens, 2 * HD), BF16),) + (piece,) * 4,
        (where, query_second[0, 0], key_second[0, 0], value_second[0, 0]),
        name="open_second",
    )
    kv1, other, packed = lax.optimization_barrier((kv1, other, packed))
    kv = swap(packed, SEQ).reshape(length, 2 * HD)
    q2 = ahead(q2)
    up = call(pack_body, sds((FOUR, tokens, cols), BF16), (where, up_raw), name="pack")
    kv, up, q2 = lax.optimization_barrier((kv, up, q2))
    up = swap(up, "ylo").reshape(n, cols)
    kv_first = lax.all_gather(
        jnp.concatenate([kv1, other], axis=0), ROW, axis=0, tiled=True
    )

    turned = pltpu.VMEM((HD, length), BF16)
    bias = pltpu.VMEM((length, n), F32)
    rows = pltpu.VMEM((n, cols), BF16)
    total = pltpu.VMEM((length, HD), F32)

    out2, lse = call(
        functools.partial(forward_body, heads),
        (sds((n, cols), BF16), sds((heads, n), F32)),
        (where, *q2, kv),
        [rows, turned, bias],
        micros=6.4,
        name="forward_second",
    )
    stats = swap(
        call(
            functools.partial(stats_body, heads),
            sds((FOUR, 8, n), F32),
            (where, out2, up, gain_cols),
            name="stats",
        ),
        "ylo",
    )
    *dq, dkv = call(
        functools.partial(backward_body, heads, width),
        (piece,) * 4 + (sds((places, tokens + 16, 2 * HD), BF16),),
        (where, *q2, kv, up, gain_cols, out2, lse, stats),
        [rows, turned, bias, total, total, rows],
        micros=7.0,
        name="backward",
    )
    dkv = swap(dkv, SEQ)
    dq = ahead(dq)

    normed = call(
        first_body,
        sds((tokens, width), BF16),
        (where, query_first[0, 0], kv_first, gain),
        [
            pltpu.VMEM((length, HD), BF16),
            turned,
            pltpu.VMEM((n, HD), BF16),
            pltpu.VMEM((tokens, width), BF16),
            bias,
        ],
        micros=7.0,
        name="forward_first",
    )
    next_input = along(normed, "pipe", 1, pipes)

    dkv, normed, dq = lax.optimization_barrier((dkv, normed, dq))
    grad_key, grad_value, share = call(
        gather_body,
        (sds((tokens, kv_width), BF16),) * 2 + (sds((1, 2 * HD), F32),),
        (where, dkv),
        name="gather",
    )
    grad_gain = lax.psum(share, "dp")
    grad_query = call(join_body, sds((tokens, width), BF16), (where, *dq), name="join")
    return (
        next_input[None, None],
        grad_query[None, None],
        grad_key[None, None],
        grad_value[None, None],
        grad_gain,
    )


def solution(mesh):
    shape = mesh.devices.shape
    fine = Mesh(
        mesh.devices.reshape(shape[0], shape[1], 2, 2, shape[2] // 4),
        ("dp", "pipe", "zhi", "yhi", "ylo"),
    )
    big = P("dp", "pipe", SEQ, None)
    return jax.shard_map(
        local,
        mesh=fine,
        in_specs=(big,) * 7 + (P("pipe", None),),
        out_specs=(big,) * 4 + (P("pipe", SEQ),),
        check_vma=False,
    )
```

```python
import functools
import math

import jax
import jax.numpy as jnp
from jax import lax
from jax.experimental import pallas as pl
from jax.experimental.pallas import tpu as pltpu
from jax.sharding import Mesh
from jax.sharding import PartitionSpec as P

HD = 128
EPSILON = 1e-05
SCALE = 1.0 / math.sqrt(HD)
F32 = jnp.float32
BF16 = jnp.bfloat16

ROW = ("yhi", "ylo")
SEQ = ("zhi", "yhi", "ylo")
FOUR = 4

VMEM = pl.BlockSpec(memory_space=pltpu.VMEM)
SMEM = pl.BlockSpec(memory_space=pltpu.SMEM)


def call(body, outs, inputs, scratch=(), micros=1.0, name=None):
    return pl.pallas_call(
        body,
        out_shape=outs,
        in_specs=[SMEM] + [VMEM] * (len(inputs) - 1),
        out_specs=jax.tree.map(lambda _: VMEM, outs),
        scratch_shapes=list(scratch),
        compiler_params=pltpu.CompilerParams(vmem_limit_bytes=48 * 1024 * 1024),
        cost_estimate=pl.CostEstimate(
            flops=int(micros * 1e9), bytes_accessed=0, transcendentals=0
        ),
        name=name,
    )(*inputs)


def sds(shape, dtype):
    return jax.ShapeDtypeStruct(shape, dtype)


def dot_nt(a, b):
    return lax.dot_general(a, b, (((1,), (1,)), ((), ())), preferred_element_type=F32)


def dot_nn(a, b):
    return lax.dot_general(a, b, (((1,), (0,)), ((), ())), preferred_element_type=F32)


def column(row):
    return jnp.broadcast_to(row, (HD, row.shape[1])).T


def row_of(block):
    return jnp.sum(block.T, axis=0, keepdims=True)


def attend(keys, values_t, bias, queries):
    scores = dot_nt(keys, queries) + bias[...]
    highest = jnp.max(scores, axis=0, keepdims=True)
    exponent = jnp.exp((scores - highest) * SCALE)
    total = jnp.sum(exponent, axis=0, keepdims=True)
    out = dot_nn(values_t, exponent.astype(BF16)) * (1.0 / total)
    return out.T.astype(BF16), highest * SCALE + jnp.log(total)


def set_bias(where, bias):
    shape = bias.shape
    ahead = lax.broadcasted_iota(jnp.int32, shape, 0) - lax.broadcasted_iota(jnp.int32, shape, 1)
    bias[...] = jnp.where(ahead <= where[0] * shape[1], 0.0, -jnp.inf).astype(F32)


def open_body(where, keys, values, kv):
    for s in range(kv.shape[0]):
        cols = slice((s % FOUR) * HD, (s % FOUR + 1) * HD)
        kv[s, :, :HD] = keys[:, cols]
        kv[s, :, HD:] = values[:, cols]


def pack_body(where, full, out):
    width = out.shape[2]
    for place in range(FOUR):
        out[place] = full[:, place * width : (place + 1) * width]


def join_body(where, parts, out):
    width = parts.shape[2]
    for place in range(FOUR):
        out[:, place * width : (place + 1) * width] = parts[place]


def gather_body(where, parts, keys, values, share):
    tokens = keys.shape[0]
    for h in range(FOUR):
        cols = slice(h * HD, (h + 1) * HD)
        total = parts[h, :tokens].astype(F32)
        for s in range(h + FOUR, parts.shape[0], FOUR):
            total = total + parts[s, :tokens].astype(F32)
        keys[:, cols] = total[:, :HD].astype(BF16)
        values[:, cols] = total[:, HD:].astype(BF16)
    terms = parts[0, tokens:].astype(F32)
    for s in range(1, parts.shape[0]):
        terms = terms + parts[s, tokens:].astype(F32)
    share[...] = terms[0:1] + terms[1:2] + terms[2:3]


def forward_body(heads, where, q, kv, out, lse, vt_s, bias):
    set_bias(where, bias)
    vt_s[...] = kv[:, HD:].T
    for h in range(heads):
        cols = slice(h * HD, (h + 1) * HD)
        out[:, cols], lse[h : h + 1, :] = attend(kv[:, :HD], vt_s[...], bias, q[:, cols])


def stats_body(heads, where, act, up, gain, stats):
    n = act.shape[0]
    square = jnp.zeros((n, HD), F32)
    cross = jnp.zeros((n, HD), F32)
    for h in range(heads):
        cols = slice(h * HD, (h + 1) * HD)
        value = act[:, cols].astype(F32)
        square = square + value * value
        cross = cross + gain[:, cols].astype(F32) * up[:, cols].astype(F32) * value
    rows = jnp.concatenate(
        [row_of(square), row_of(cross), jnp.zeros((stats.shape[1] - 2, n), F32)], axis=0
    )
    for place in range(FOUR):
        stats[place] = rows


def backward_body(
    heads, width, where, q, kv, up, gain, act, lse, stats,
    dq, dkv, sums, kt_s, bias, dk_s, dv_s,
):
    set_bias(where, bias)
    kt_s[...] = kv[:, :HD].T
    totals = (stats[0] + stats[1]) + (stats[2] + stats[3])
    inverse_row = lax.rsqrt(totals[0:1] / width + EPSILON)
    inverse = column(inverse_row)
    shrink = column(inverse_row * inverse_row * inverse_row * (totals[1:2] / width))
    per = heads // FOUR
    for h in range(heads):
        cols = slice(h * HD, (h + 1) * HD)
        queries = q[:, cols]
        act_h = act[:, cols].astype(F32)
        upstream = up[:, cols].astype(F32)
        sums[h // per : h // per + 1, (h % per) * HD : (h % per + 1) * HD] = jnp.sum(
            upstream * act_h * inverse, axis=0, keepdims=True
        )
        grad = (gain[:, cols].astype(F32) * upstream * inverse - act_h * shrink).astype(BF16)
        dots = row_of(grad.astype(F32) * act_h)
        scores = dot_nt(kv[:, :HD], queries) * SCALE + bias[...]
        probs = jnp.exp(scores - lse[h : h + 1, :])
        grad_weights = dot_nt(kv[:, HD:], grad)
        grad_scores = (probs * (grad_weights - dots) * SCALE).astype(BF16)
        dv = dot_nn(probs.astype(BF16), grad)
        dk = dot_nn(grad_scores, queries)
        if h == 0:
            dv_s[...] = dv
            dk_s[...] = dk
        else:
            dv_s[...] += dv
            dk_s[...] += dk
        dq[:, cols] = dot_nn(kt_s[...], grad_scores).T.astype(BF16)
    tokens = dk_s.shape[0] // dkv.shape[0]
    for s in range(dkv.shape[0]):
        rows = slice(s * tokens, (s + 1) * tokens)
        dkv[s, :tokens, :HD] = dk_s[rows].astype(BF16)
        dkv[s, :tokens, HD:] = dv_s[rows].astype(BF16)
        dkv[s, tokens:, :] = jnp.zeros((dkv.shape[1] - tokens, 2 * HD), BF16)


def insert_body(where, sums, dkv, out):
    del dkv
    for s in range(out.shape[0]):
        value = sums[s % FOUR : s % FOUR + 1]
        value = jnp.where(where[2] == s // FOUR, value, 0.0)
        terms = []
        for _ in range(3):
            term = value.astype(BF16).astype(F32)
            terms.append(term)
            value = value - term
        terms.append(jnp.zeros((out.shape[1] - 3, value.shape[1]), F32))
        out[s] = jnp.concatenate(terms, axis=0).astype(BF16)


def first_body(where, q, kv, gain, out, k_s, vt_s, q_s, o_s, bias):
    tokens, width = q.shape
    length = kv.shape[0]
    kv_heads = kv.shape[1] // (2 * HD)
    heads = width // HD
    n = bias.shape[1]
    together = n // tokens
    ids = lax.broadcasted_iota(jnp.int32, (length, n), 0)
    query_ids = lax.broadcasted_iota(jnp.int32, (length, n), 1) % tokens
    block = ids // tokens
    half = (block % 2 + where[1]) % 2
    key_at = half * (length // 2) + (block // 2) * tokens + ids % tokens
    query_at = where[1] * (length // 2) + where[3] * tokens + query_ids
    bias[...] = jnp.where(key_at <= query_at, 0.0, -jnp.inf).astype(F32)
    square = jnp.zeros((tokens, HD), F32)
    for g in range(kv_heads):
        k_s[...] = kv[:, g * HD : (g + 1) * HD]
        vt_s[...] = kv[:, (kv_heads + g) * HD : (kv_heads + g + 1) * HD].T
        for part in range(heads // kv_heads // together):
            start = g * (heads // kv_heads) + part * together
            for i in range(together):
                q_s[i * tokens : (i + 1) * tokens, :] = q[:, (start + i) * HD : (start + i + 1) * HD]
            result, _ = attend(k_s[...], vt_s[...], bias, q_s[...])
            for i in range(together):
                piece = result[i * tokens : (i + 1) * tokens]
                o_s[:, (start + i) * HD : (start + i + 1) * HD] = piece
                piece = piece.astype(F32)
                square = square + piece * piece
    mean = jnp.sum(square, axis=1, keepdims=True) / width
    inverse = jnp.broadcast_to(lax.rsqrt(mean + EPSILON), (tokens, HD))
    for h in range(heads):
        cols = slice(h * HD, (h + 1) * HD)
        out[:, cols] = (gain[:, cols].astype(F32) * o_s[:, cols].astype(F32) * inverse).astype(BF16)


def local(
    query_first, key_first, value_first, query_second, key_second, value_second, grad_output, gain
):
    tokens, width = query_first.shape[2:]
    kv_width = key_first.shape[3]
    n = tokens * FOUR
    cols = width // FOUR
    heads = cols // HD
    places = lax.axis_size(SEQ)
    length = tokens * places
    pipes = lax.axis_size("pipe")
    zhi, yhi, ylo = (lax.axis_index(axis) for axis in SEQ)
    where = jnp.stack([zhi * 2 + yhi, zhi, ylo, yhi * FOUR + ylo]).astype(jnp.int32)
    gain_cols = lax.dynamic_slice_in_dim(gain, ylo * cols, cols, 1)

    def swap(packed, axes):
        return lax.all_to_all(packed, axes, split_axis=0, concat_axis=0, tiled=True)

    def along(value, axis, step, count):
        return lax.ppermute(value, axis, [(i, (i + step) % count) for i in range(count)])

    up_raw = along(grad_output[0, 0], "pipe", -1, pipes)
    kv1 = jnp.concatenate([key_first[0, 0], value_first[0, 0]], axis=1)
    def by_heads(full):
        return call(pack_body, sds((FOUR, tokens, cols), BF16), (where, full), micros=1.4, name="pack")

    q2 = swap(by_heads(query_second[0, 0]), "ylo")
    packed = call(
        open_body,
        sds((places, tokens, 2 * HD), BF16),
        (where, key_second[0, 0], value_second[0, 0]),
        name="open_second",
    )
    up = by_heads(up_raw)
    other = lax.ppermute(kv1, "zhi", [(0, 1)])
    packed, q2, up, other = lax.optimization_barrier((packed, q2, up, other))
    q2 = q2.reshape(n, cols)
    kv = swap(packed, SEQ).reshape(length, 2 * HD)
    kv, up = lax.optimization_barrier((kv, up))
    up = swap(up, "ylo").reshape(n, cols)
    kv1, other, kv = lax.optimization_barrier((kv1, other, kv))
    kv_first = lax.all_gather(
        jnp.concatenate([kv1, other], axis=0), ROW, axis=0, tiled=True
    )

    turned = pltpu.VMEM((HD, length), BF16)
    bias = pltpu.VMEM((length, n), F32)
    total = pltpu.VMEM((length, HD), F32)

    out2, lse = call(
        functools.partial(forward_body, heads),
        (sds((n, cols), BF16), sds((heads, n), F32)),
        (where, q2, kv),
        [turned, bias],
        micros=6.4,
        name="forward_second",
    )
    stats = swap(
        call(
            functools.partial(stats_body, heads),
            sds((FOUR, 8, n), F32),
            (where, out2, up, gain_cols),
            name="stats",
        ),
        "ylo",
    )
    dq, dkv, sums = call(
        functools.partial(backward_body, heads, width),
        (
            sds((n, cols), BF16),
            sds((places, tokens + 16, 2 * HD), BF16),
            sds((FOUR, 2 * HD), F32),
        ),
        (where, q2, kv, up, gain_cols, out2, lse, stats),
        [turned, bias, total, total],
        micros=7.0,
        name="backward",
    )
    dq = swap(dq.reshape(FOUR, tokens, cols), "ylo")
    sums = lax.psum(sums, "dp")
    below = pl.BlockSpec((places, 16, 2 * HD), lambda i: (0, tokens // 16, 0))
    dkv = pl.pallas_call(
        insert_body,
        grid=(1,),
        in_specs=[SMEM, pl.BlockSpec((FOUR, 2 * HD), lambda i: (0, 0)), below],
        out_specs=below,
        out_shape=sds(dkv.shape, BF16),
        input_output_aliases={2: 0},
        cost_estimate=pl.CostEstimate(flops=10**9, bytes_accessed=0, transcendentals=0),
        name="insert",
    )(where, sums, dkv)
    dkv, dq = lax.optimization_barrier((dkv, dq))
    dkv = swap(dkv, SEQ)

    normed = call(
        first_body,
        sds((tokens, width), BF16),
        (where, query_first[0, 0], kv_first, gain),
        [
            pltpu.VMEM((length, HD), BF16),
            turned,
            pltpu.VMEM((n, HD), BF16),
            pltpu.VMEM((tokens, width), BF16),
            bias,
        ],
        micros=7.0,
        name="forward_first",
    )
    next_input = along(normed, "pipe", 1, pipes)
    grad_key, grad_value, share = call(
        gather_body,
        (sds((tokens, kv_width), BF16),) * 2 + (sds((1, 2 * HD), F32),),
        (where, dkv),
        name="gather",
    )
    grad_gain = share
    grad_query = call(join_body, sds((tokens, width), BF16), (where, dq), name="join")
    return (
        next_input[None, None],
        grad_query[None, None],
        grad_key[None, None],
        grad_value[None, None],
        grad_gain,
    )


def solution(mesh):
    shape = mesh.devices.shape
    fine = Mesh(
        mesh.devices.reshape(shape[0], shape[1], 2, 2, shape[2] // 4),
        ("dp", "pipe", "zhi", "yhi", "ylo"),
    )
    big = P("dp", "pipe", SEQ, None)
    return jax.shard_map(
        local,
        mesh=fine,
        in_specs=(big,) * 7 + (P("pipe", None),),
        out_specs=(big,) * 4 + (P("pipe", SEQ),),
        check_vma=False,
    )
```

```python
import functools
import math

import jax
import jax.numpy as jnp
from jax import lax
from jax.experimental import pallas as pl
from jax.experimental.pallas import tpu as pltpu
from jax.sharding import Mesh
from jax.sharding import PartitionSpec as P

HD = 128
EPSILON = 1e-05
SCALE = 1.0 / math.sqrt(HD)
F32 = jnp.float32
BF16 = jnp.bfloat16

ROW = ("yhi", "ylo")
SEQ = ("zhi", "yhi", "ylo")
FOUR = 4

VMEM = pl.BlockSpec(memory_space=pltpu.VMEM)
SMEM = pl.BlockSpec(memory_space=pltpu.SMEM)


def call(body, outs, inputs, scratch=(), micros=1.0, name=None):
    return pl.pallas_call(
        body,
        out_shape=outs,
        in_specs=[SMEM] + [VMEM] * (len(inputs) - 1),
        out_specs=jax.tree.map(lambda _: VMEM, outs),
        scratch_shapes=list(scratch),
        compiler_params=pltpu.CompilerParams(vmem_limit_bytes=48 * 1024 * 1024),
        cost_estimate=pl.CostEstimate(
            flops=int(micros * 1e9), bytes_accessed=0, transcendentals=0
        ),
        name=name,
    )(*inputs)


def sds(shape, dtype):
    return jax.ShapeDtypeStruct(shape, dtype)


def dot_nt(a, b):
    return lax.dot_general(a, b, (((1,), (1,)), ((), ())), preferred_element_type=F32)


def dot_nn(a, b):
    return lax.dot_general(a, b, (((1,), (0,)), ((), ())), preferred_element_type=F32)


def column(row):
    return jnp.broadcast_to(row, (HD, row.shape[1])).T


def row_of(block):
    return jnp.sum(block.T, axis=0, keepdims=True)


def head_at(where, place):
    return place + where[4] * (FOUR - 1 - 2 * place)


def head_columns(where, place, width):
    return pl.ds(pl.multiple_of(head_at(where, place) * width, width), width)


def attend(keys, values_t, bias, queries):
    scores = dot_nt(keys, queries) + bias[...]
    highest = jnp.max(scores, axis=0, keepdims=True)
    exponent = jnp.exp((scores - highest) * SCALE)
    total = jnp.sum(exponent, axis=0, keepdims=True)
    out = dot_nn(values_t, exponent.astype(BF16)) * (1.0 / total)
    return out.T.astype(BF16), highest * SCALE + jnp.log(total)


def set_bias(where, bias):
    shape = bias.shape
    ahead = lax.broadcasted_iota(jnp.int32, shape, 0) - lax.broadcasted_iota(jnp.int32, shape, 1)
    bias[...] = jnp.where(ahead <= where[0] * shape[1], 0.0, -jnp.inf).astype(F32)


def load_keys(where, blocks, at, full):
    n = blocks[0].shape[0]
    for i, block in enumerate(blocks):
        group = where[0] if i == 0 else where[4 + i]
        full[pl.ds(pl.multiple_of(group * n, n), n), :] = block[:, at : at + HD]


def open_body(where, query, keys, values, out):
    width = query.shape[1] // FOUR
    for place in range(FOUR):
        cols = head_columns(where, place, HD)
        out[place, :, :width] = query[:, head_columns(where, place, width)]
        out[place, :, width : width + HD] = keys[:, cols]
        out[place, :, width + HD :] = values[:, cols]


def pack_body(where, full, out):
    for place in range(FOUR):
        out[place] = full[:, head_columns(where, place, out.shape[2])]


def join_body(where, parts, out):
    for place in range(FOUR):
        out[:, head_columns(where, place, parts.shape[2])] = parts[place]


def gather_body(where, parts, keys, values, share):
    tokens = keys.shape[0]
    for h in range(FOUR):
        cols = slice(h * HD, (h + 1) * HD)
        total = 0.0
        for group in range(parts.shape[0] // FOUR):
            place = FOUR - 1 - h if group % 2 else h
            total = total + parts[group * FOUR + place, :tokens].astype(F32)
        keys[:, cols] = total[:, :HD].astype(BF16)
        values[:, cols] = total[:, HD:].astype(BF16)
    terms = parts[0, tokens:].astype(F32)
    for s in range(1, parts.shape[0]):
        terms = terms + parts[s, tokens:].astype(F32)
    share[...] = terms[0:1] + terms[1:2] + terms[2:3]


def forward_body(heads, where, q, kv1, kv2, kv3, out, lse, k_s, v_s, bias):
    set_bias(where, bias)
    blocks = (q.at[:, heads * HD :], kv1, kv2, kv3)
    load_keys(where, blocks, 0, k_s)
    load_keys(where, blocks, HD, v_s)
    values_t = v_s[...].T
    for h in range(heads):
        cols = slice(h * HD, (h + 1) * HD)
        out[:, cols], lse[h : h + 1, :] = attend(k_s[...], values_t, bias, q[:, cols])


def stats_body(heads, where, act, up, gain, stats):
    n = act.shape[0]
    square = jnp.zeros((n, HD), F32)
    cross = jnp.zeros((n, HD), F32)
    for h in range(heads):
        cols = slice(h * HD, (h + 1) * HD)
        value = act[:, cols].astype(F32)
        square = square + value * value
        cross = cross + gain[:, cols].astype(F32) * up[:, cols].astype(F32) * value
    rows = jnp.concatenate(
        [row_of(square), row_of(cross), jnp.zeros((stats.shape[1] - 2, n), F32)], axis=0
    )
    for place in range(FOUR):
        stats[place] = rows


def backward_body(
    heads, width, where, q, kv1, kv2, kv3, up, gain, act, lse, stats,
    dq, dkv, sums, k_s, v_s, bias, dk_s, dv_s,
):
    set_bias(where, bias)
    blocks = (q.at[:, heads * HD :], kv1, kv2, kv3)
    load_keys(where, blocks, 0, k_s)
    load_keys(where, blocks, HD, v_s)
    keys_t = k_s[...].T
    totals = (stats[0] + stats[1]) + (stats[2] + stats[3])
    inverse_row = lax.rsqrt(totals[0:1] / width + EPSILON)
    inverse = column(inverse_row)
    shrink = column(inverse_row * inverse_row * inverse_row * (totals[1:2] / width))
    per = heads // FOUR
    for h in range(heads):
        cols = slice(h * HD, (h + 1) * HD)
        queries = q[:, cols]
        act_h = act[:, cols].astype(F32)
        upstream = up[:, cols].astype(F32)
        sums[h // per : h // per + 1, (h % per) * HD : (h % per + 1) * HD] = jnp.sum(
            upstream * act_h * inverse, axis=0, keepdims=True
        )
        grad = (gain[:, cols].astype(F32) * upstream * inverse - act_h * shrink).astype(BF16)
        dots = row_of(grad.astype(F32) * act_h)
        scores = dot_nt(k_s[...], queries) * SCALE + bias[...]
        probs = jnp.exp(scores - lse[h : h + 1, :])
        grad_weights = dot_nt(v_s[...], grad)
        grad_scores = (probs * (grad_weights - dots) * SCALE).astype(BF16)
        dv = dot_nn(probs.astype(BF16), grad)
        dk = dot_nn(grad_scores, queries)
        if h == 0:
            dv_s[...] = dv
            dk_s[...] = dk
        else:
            dv_s[...] += dv
            dk_s[...] += dk
        dq[:, cols] = dot_nn(keys_t, grad_scores).T.astype(BF16)
    tokens = dk_s.shape[0] // dkv.shape[0]
    for s in range(dkv.shape[0]):
        rows = slice(s * tokens, (s + 1) * tokens)
        dkv[s, :tokens, :HD] = dk_s[rows].astype(BF16)
        dkv[s, :tokens, HD:] = dv_s[rows].astype(BF16)
        dkv[s, tokens:, :] = jnp.zeros((dkv.shape[1] - tokens, 2 * HD), BF16)


def insert_body(where, sums, dkv, out):
    del dkv
    for s in range(out.shape[0]):
        value = sums[s % FOUR : s % FOUR + 1]
        value = jnp.where(where[2] == s // FOUR, value, 0.0)
        terms = []
        for _ in range(3):
            term = value.astype(BF16).astype(F32)
            terms.append(term)
            value = value - term
        terms.append(jnp.zeros((out.shape[1] - 3, value.shape[1]), F32))
        out[s] = jnp.concatenate(terms, axis=0).astype(BF16)


def first_body(where, q, kv, gain, out, k_s, vt_s, q_s, o_s, bias):
    tokens, width = q.shape
    length = kv.shape[0]
    kv_heads = kv.shape[1] // (2 * HD)
    heads = width // HD
    n = bias.shape[1]
    together = n // tokens
    ids = lax.broadcasted_iota(jnp.int32, (length, n), 0)
    query_ids = lax.broadcasted_iota(jnp.int32, (length, n), 1) % tokens
    block = ids // tokens
    half = (block % 2 + where[1]) % 2
    key_at = half * (length // 2) + (block // 2) * tokens + ids % tokens
    query_at = where[1] * (length // 2) + where[3] * tokens + query_ids
    bias[...] = jnp.where(key_at <= query_at, 0.0, -jnp.inf).astype(F32)
    square = jnp.zeros((tokens, HD), F32)
    for g in range(kv_heads):
        k_s[...] = kv[:, g * HD : (g + 1) * HD]
        vt_s[...] = kv[:, (kv_heads + g) * HD : (kv_heads + g + 1) * HD].T
        for part in range(heads // kv_heads // together):
            start = g * (heads // kv_heads) + part * together
            for i in range(together):
                q_s[i * tokens : (i + 1) * tokens, :] = q[:, (start + i) * HD : (start + i + 1) * HD]
            result, _ = attend(k_s[...], vt_s[...], bias, q_s[...])
            for i in range(together):
                piece = result[i * tokens : (i + 1) * tokens]
                o_s[:, (start + i) * HD : (start + i + 1) * HD] = piece
                piece = piece.astype(F32)
                square = square + piece * piece
    mean = jnp.sum(square, axis=1, keepdims=True) / width
    inverse = jnp.broadcast_to(lax.rsqrt(mean + EPSILON), (tokens, HD))
    for h in range(heads):
        cols = slice(h * HD, (h + 1) * HD)
        out[:, cols] = (gain[:, cols].astype(F32) * o_s[:, cols].astype(F32) * inverse).astype(BF16)


def local(
    query_first, key_first, value_first, query_second, key_second, value_second, grad_output, gain
):
    tokens, width = query_first.shape[2:]
    kv_width = key_first.shape[3]
    n = tokens * FOUR
    cols = width // FOUR
    heads = cols // HD
    places = lax.axis_size(SEQ)
    length = tokens * places
    pipes = lax.axis_size("pipe")
    zhi, yhi, ylo = (lax.axis_index(axis) for axis in SEQ)
    group = zhi * 2 + yhi
    mine = ylo + yhi * (FOUR - 1 - 2 * ylo)
    where = jnp.stack(
        [group, zhi, mine, yhi * FOUR + ylo, yhi, zhi * 2 + 1 - yhi, 2 - zhi * 2 + yhi, 3 - group]
    ).astype(jnp.int32)
    gain_cols = lax.dynamic_slice_in_dim(gain, mine * cols, cols, 1)

    def device(z, h, y):
        return (z * 2 + h) * FOUR + y

    near = [(device(z, 0, y), device(z, 1, 3 - y)) for z in range(2) for y in range(FOUR)]
    far = [(device(0, h, y), device(1, h, y)) for h in range(2) for y in range(FOUR)]
    cross = [(device(0, h, y), device(1, 1 - h, 3 - y)) for h in range(2) for y in range(FOUR)]

    def swap(packed, axes):
        return lax.all_to_all(packed, axes, split_axis=0, concat_axis=0, tiled=True)

    def along(value, axis, step, count):
        return lax.ppermute(value, axis, [(i, (i + step) % count) for i in range(count)])

    up_raw = along(grad_output[0, 0], "pipe", -1, pipes)
    kv1 = jnp.concatenate([key_first[0, 0], value_first[0, 0]], axis=1)
    other = lax.ppermute(kv1, "zhi", [(0, 1)])
    qkv = call(
        open_body,
        sds((FOUR, tokens, cols + 2 * HD), BF16),
        (where, query_second[0, 0], key_second[0, 0], value_second[0, 0]),
        name="open_second",
    )
    qkv = swap(qkv, "ylo")
    up = call(
        pack_body, sds((FOUR, tokens, cols), BF16), (where, up_raw), micros=1.4, name="pack"
    )
    qkv, up, other = lax.optimization_barrier((qkv, up, other))
    qkv = qkv.reshape(n, cols + 2 * HD)
    kvs = [lax.ppermute(qkv[:, cols:], SEQ, pairs) for pairs in (near, far, cross)]
    up = swap(up, "ylo").reshape(n, cols)
    kv_first = lax.all_gather(
        jnp.concatenate([kv1, other], axis=0), ROW, axis=0, tiled=True
    )

    long = pltpu.VMEM((length, HD), BF16)
    turned = pltpu.VMEM((HD, length), BF16)
    bias = pltpu.VMEM((length, n), F32)
    total = pltpu.VMEM((length, HD), F32)

    out2, lse = call(
        functools.partial(forward_body, heads),
        (sds((n, cols), BF16), sds((heads, n), F32)),
        (where, qkv, *kvs),
        [long, long, bias],
        micros=6.4,
        name="forward_second",
    )
    stats = swap(
        call(
            functools.partial(stats_body, heads),
            sds((FOUR, 8, n), F32),
            (where, out2, up, gain_cols),
            name="stats",
        ),
        "ylo",
    )
    dq, dkv, sums = call(
        functools.partial(backward_body, heads, width),
        (
            sds((n, cols), BF16),
            sds((places, tokens + 16, 2 * HD), BF16),
            sds((FOUR, 2 * HD), F32),
        ),
        (where, qkv, *kvs, up, gain_cols, out2, lse, stats),
        [long, long, bias, total, total],
        micros=7.0,
        name="backward",
    )
    dq = swap(dq.reshape(FOUR, tokens, cols), "ylo")
    sums = lax.psum(sums, "dp")
    below = pl.BlockSpec((places, 16, 2 * HD), lambda i: (0, tokens // 16, 0))
    dkv = pl.pallas_call(
        insert_body,
        grid=(1,),
        in_specs=[SMEM, pl.BlockSpec((FOUR, 2 * HD), lambda i: (0, 0)), below],
        out_specs=below,
        out_shape=sds(dkv.shape, BF16),
        input_output_aliases={2: 0},
        cost_estimate=pl.CostEstimate(flops=10**9, bytes_accessed=0, transcendentals=0),
        name="insert",
    )(where, sums, dkv)
    dkv, dq = lax.optimization_barrier((dkv, dq))
    dkv = swap(dkv, SEQ)

    normed = call(
        first_body,
        sds((tokens, width), BF16),
        (where, query_first[0, 0], kv_first, gain),
        [
            long,
            turned,
            pltpu.VMEM((n, HD), BF16),
            pltpu.VMEM((tokens, width), BF16),
            bias,
        ],
        micros=7.0,
        name="forward_first",
    )
    next_input = along(normed, "pipe", 1, pipes)
    grad_key, grad_value, share = call(
        gather_body,
        (sds((tokens, kv_width), BF16),) * 2 + (sds((1, 2 * HD), F32),),
        (where, dkv),
        name="gather",
    )
    grad_gain = share
    grad_query = call(join_body, sds((tokens, width), BF16), (where, dq), name="join")
    return (
        next_input[None, None],
        grad_query[None, None],
        grad_key[None, None],
        grad_value[None, None],
        grad_gain,
    )


def solution(mesh):
    shape = mesh.devices.shape
    fine = Mesh(
        mesh.devices.reshape(shape[0], shape[1], 2, 2, shape[2] // 4),
        ("dp", "pipe", "zhi", "yhi", "ylo"),
    )
    big = P("dp", "pipe", SEQ, None)
    return jax.shard_map(
        local,
        mesh=fine,
        in_specs=(big,) * 7 + (P("pipe", None),),
        out_specs=(big,) * 4 + (P("pipe", SEQ),),
        check_vma=False,
    )
```

```python
import functools
import math

import jax
import jax.numpy as jnp
from jax import lax
from jax.experimental import pallas as pl
from jax.experimental.pallas import tpu as pltpu
from jax.sharding import Mesh
from jax.sharding import PartitionSpec as P

HD = 128
EPSILON = 1e-05
SCALE = 1.0 / math.sqrt(HD)
BINARY = SCALE / math.log(2.0)
F32 = jnp.float32
BF16 = jnp.bfloat16

ROW = ("yhi", "ylo")
SEQ = ("zhi", "yhi", "ylo")
FOUR = 4

VMEM = pl.BlockSpec(memory_space=pltpu.VMEM)
SMEM = pl.BlockSpec(memory_space=pltpu.SMEM)


def call(body, outs, inputs, scratch=(), micros=1.0, name=None):
    return pl.pallas_call(
        body,
        out_shape=outs,
        in_specs=[SMEM] + [VMEM] * (len(inputs) - 1),
        out_specs=jax.tree.map(lambda _: VMEM, outs),
        scratch_shapes=list(scratch),
        compiler_params=pltpu.CompilerParams(vmem_limit_bytes=48 * 1024 * 1024),
        cost_estimate=pl.CostEstimate(
            flops=int(micros * 1e9), bytes_accessed=0, transcendentals=0
        ),
        name=name,
    )(*inputs)


def sds(shape, dtype):
    return jax.ShapeDtypeStruct(shape, dtype)


def dot_nt(a, b):
    return lax.dot_general(a, b, (((1,), (1,)), ((), ())), preferred_element_type=F32)


def dot_nn(a, b):
    return lax.dot_general(a, b, (((1,), (0,)), ((), ())), preferred_element_type=F32)


def column(row):
    return jnp.broadcast_to(row, (HD, row.shape[1])).T


def row_of(block):
    return jnp.sum(block.T, axis=0, keepdims=True)


def head_at(where, place):
    return place + where[4] * (FOUR - 1 - 2 * place)


def head_columns(where, place, width):
    return pl.ds(pl.multiple_of(head_at(where, place) * width, width), width)


def attend(scores, values_t, bias):
    scores = scores + bias[...]
    highest = jnp.max(scores, axis=0, keepdims=True)
    exponent = jnp.exp2((scores - highest) * BINARY)
    total = jnp.sum(exponent, axis=0, keepdims=True)
    out = dot_nn(values_t, exponent.astype(BF16)) * (1.0 / total)
    return out.T.astype(BF16), highest * BINARY + jnp.log2(total)


def ahead_of(count, make):
    after = make(0)
    for i in range(count):
        now = after
        if i + 1 < count:
            after = make(i + 1)
        yield i, now


def set_bias(where, bias):
    shape = bias.shape
    ahead = lax.broadcasted_iota(jnp.int32, shape, 0) - lax.broadcasted_iota(jnp.int32, shape, 1)
    bias[...] = jnp.where(ahead <= where[0] * shape[1], 0.0, -jnp.inf).astype(F32)


def load_keys(where, blocks, at, full):
    n = blocks[0].shape[0]
    for i, block in enumerate(blocks):
        group = where[0] if i == 0 else where[4 + i]
        full[pl.ds(pl.multiple_of(group * n, n), n), :] = block[:, at : at + HD]


def open_body(where, query, keys, values, out):
    width = query.shape[1] // FOUR
    for place in range(FOUR):
        cols = head_columns(where, place, HD)
        out[place, :, :width] = query[:, head_columns(where, place, width)]
        out[place, :, width : width + HD] = keys[:, cols]
        out[place, :, width + HD :] = values[:, cols]


def pack_body(where, full, out):
    for place in range(FOUR):
        out[place] = full[:, head_columns(where, place, out.shape[2])]


def join_body(where, parts, out):
    for place in range(FOUR):
        out[:, head_columns(where, place, parts.shape[2])] = parts[place]


def gather_body(where, parts, keys, values, share):
    tokens = keys.shape[0]
    for h in range(FOUR):
        cols = slice(h * HD, (h + 1) * HD)
        total = 0.0
        for group in range(parts.shape[0] // FOUR):
            place = FOUR - 1 - h if group % 2 else h
            total = total + parts[group * FOUR + place, :tokens].astype(F32)
        keys[:, cols] = total[:, :HD].astype(BF16)
        values[:, cols] = total[:, HD:].astype(BF16)
    terms = parts[0, tokens:].astype(F32)
    for s in range(1, parts.shape[0]):
        terms = terms + parts[s, tokens:].astype(F32)
    share[...] = terms[0:1] + terms[1:2] + terms[2:3]


def forward_body(heads, where, q, kv1, kv2, kv3, up, gain, out, lse, stats, k_s, v_s, bias):
    set_bias(where, bias)
    blocks = (q.at[:, heads * HD :], kv1, kv2, kv3)
    load_keys(where, blocks, 0, k_s)
    load_keys(where, blocks, HD, v_s)
    values_t = v_s[...].T
    n = bias.shape[1]
    square = jnp.zeros((n, HD), F32)
    cross = jnp.zeros((n, HD), F32)
    for h, scores in ahead_of(heads, lambda h: dot_nt(k_s[...], q[:, h * HD : (h + 1) * HD])):
        cols = slice(h * HD, (h + 1) * HD)
        result, lse[h : h + 1, :] = attend(scores, values_t, bias)
        out[:, cols] = result
        value = result.astype(F32)
        square = square + value * value
        cross = cross + gain[:, cols].astype(F32) * up[:, cols].astype(F32) * value
    rows = jnp.concatenate(
        [row_of(square), row_of(cross), jnp.zeros((stats.shape[1] - 2, n), F32)], axis=0
    )
    for place in range(FOUR):
        stats[place] = rows


def backward_body(
    heads, width, where, q, kv1, kv2, kv3, up, gain, act, lse, stats,
    dq, dkv, k_s, v_s, bias, dk_s, dv_s,
):
    set_bias(where, bias)
    blocks = (q.at[:, heads * HD :], kv1, kv2, kv3)
    load_keys(where, blocks, 0, k_s)
    load_keys(where, blocks, HD, v_s)
    keys_t = k_s[...].T
    totals = (stats[0] + stats[1]) + (stats[2] + stats[3])
    inverse_row = lax.rsqrt(totals[0:1] / width + EPSILON)
    inverse = column(inverse_row)
    shrink = column(inverse_row * inverse_row * inverse_row * (totals[1:2] / width))
    sums = []
    for h in range(heads):
        cols = slice(h * HD, (h + 1) * HD)
        queries = q[:, cols]
        act_h = act[:, cols].astype(F32)
        upstream = up[:, cols].astype(F32)
        sums.append(jnp.sum(upstream * act_h * inverse, axis=0, keepdims=True))
        grad = (gain[:, cols].astype(F32) * upstream * inverse - act_h * shrink).astype(BF16)
        dots = row_of(grad.astype(F32) * act_h)
        scores = dot_nt(k_s[...], queries) * BINARY + bias[...]
        probs = jnp.exp2(scores - lse[h : h + 1, :])
        grad_weights = dot_nt(v_s[...], grad)
        grad_scores = (probs * (grad_weights - dots) * SCALE).astype(BF16)
        dv = dot_nn(probs.astype(BF16), grad)
        dk = dot_nn(grad_scores, queries)
        if h == 0:
            dv_s[...] = dv
            dk_s[...] = dk
        else:
            dv_s[...] += dv
            dk_s[...] += dk
        dq[:, cols] = dot_nn(keys_t, grad_scores).T.astype(BF16)
    tokens = dk_s.shape[0] // dkv.shape[0]
    per = heads // FOUR
    extra = dkv.shape[1] - tokens
    for s in range(dkv.shape[0]):
        rows = slice(s * tokens, (s + 1) * tokens)
        dkv[s, :tokens, :HD] = dk_s[rows].astype(BF16)
        dkv[s, :tokens, HD:] = dv_s[rows].astype(BF16)
        j = s % FOUR
        value = jnp.concatenate(sums[j * per : (j + 1) * per], axis=1)
        value = jnp.where(where[2] == s // FOUR, value, 0.0)
        terms = []
        for _ in range(3):
            term = value.astype(BF16).astype(F32)
            terms.append(term)
            value = value - term
        terms.append(jnp.zeros((extra - 3, value.shape[1]), F32))
        dkv[s, tokens:] = jnp.concatenate(terms, axis=0).astype(BF16)


def first_body(where, q, kv, gain, out, k_s, vt_s, q_s, o_s, bias):
    tokens, width = q.shape
    length = kv.shape[0]
    kv_heads = kv.shape[1] // (2 * HD)
    heads = width // HD
    n = bias.shape[1]
    together = n // tokens
    ids = lax.broadcasted_iota(jnp.int32, (length, n), 0)
    query_ids = lax.broadcasted_iota(jnp.int32, (length, n), 1) % tokens
    block = ids // tokens
    half = (block % 2 + where[1]) % 2
    key_at = half * (length // 2) + (block // 2) * tokens + ids % tokens
    query_at = where[1] * (length // 2) + where[3] * tokens + query_ids
    bias[...] = jnp.where(key_at <= query_at, 0.0, -jnp.inf).astype(F32)
    square = jnp.zeros((tokens, HD), F32)
    for g in range(kv_heads):
        k_s[...] = kv[:, g * HD : (g + 1) * HD]
        vt_s[...] = kv[:, (kv_heads + g) * HD : (kv_heads + g + 1) * HD].T
        for part in range(heads // kv_heads // together):
            start = g * (heads // kv_heads) + part * together
            for i in range(together):
                q_s[i * tokens : (i + 1) * tokens, :] = q[:, (start + i) * HD : (start + i + 1) * HD]
            result, _ = attend(dot_nt(k_s[...], q_s[...]), vt_s[...], bias)
            for i in range(together):
                piece = result[i * tokens : (i + 1) * tokens]
                o_s[:, (start + i) * HD : (start + i + 1) * HD] = piece
                piece = piece.astype(F32)
                square = square + piece * piece
    mean = jnp.sum(square, axis=1, keepdims=True) / width
    inverse = jnp.broadcast_to(lax.rsqrt(mean + EPSILON), (tokens, HD))
    for h in range(heads):
        cols = slice(h * HD, (h + 1) * HD)
        out[:, cols] = (gain[:, cols].astype(F32) * o_s[:, cols].astype(F32) * inverse).astype(BF16)


def local(
    query_first, key_first, value_first, query_second, key_second, value_second, grad_output, gain
):
    tokens, width = query_first.shape[2:]
    kv_width = key_first.shape[3]
    n = tokens * FOUR
    cols = width // FOUR
    heads = cols // HD
    places = lax.axis_size(SEQ)
    length = tokens * places
    pipes = lax.axis_size("pipe")
    zhi, yhi, ylo = (lax.axis_index(axis) for axis in SEQ)
    group = zhi * 2 + yhi
    mine = ylo + yhi * (FOUR - 1 - 2 * ylo)
    where = jnp.stack(
        [group, zhi, mine, yhi * FOUR + ylo, yhi, zhi * 2 + 1 - yhi, 2 - zhi * 2 + yhi, 3 - group]
    ).astype(jnp.int32)
    gain_cols = lax.dynamic_slice_in_dim(gain, mine * cols, cols, 1)

    def device(z, h, y):
        return (z * 2 + h) * FOUR + y

    near = [(device(z, 0, y), device(z, 1, 3 - y)) for z in range(2) for y in range(FOUR)]
    far = [(device(0, h, y), device(1, h, y)) for h in range(2) for y in range(FOUR)]
    cross = [(device(0, h, y), device(1, 1 - h, 3 - y)) for h in range(2) for y in range(FOUR)]

    def swap(packed, axes):
        return lax.all_to_all(packed, axes, split_axis=0, concat_axis=0, tiled=True)

    def along(value, axis, step, count):
        return lax.ppermute(value, axis, [(i, (i + step) % count) for i in range(count)])

    up_raw = along(grad_output[0, 0], "pipe", -1, pipes)
    kv1 = jnp.concatenate([key_first[0, 0], value_first[0, 0]], axis=1)
    other = lax.ppermute(kv1, "zhi", [(0, 1)])
    qkv = pl.pallas_call(
        open_body,
        grid=(1,),
        in_specs=[
            SMEM,
            pl.BlockSpec((tokens, width), lambda i: (0, 0)),
            pl.BlockSpec((tokens, kv_width), lambda i: (0, 0)),
            pl.BlockSpec((tokens, kv_width), lambda i: (0, 0)),
        ],
        out_specs=pl.BlockSpec((FOUR, tokens, cols + 2 * HD), lambda i: (0, 0, 0)),
        out_shape=sds((FOUR, tokens, cols + 2 * HD), BF16),
        cost_estimate=pl.CostEstimate(flops=10**9, bytes_accessed=0, transcendentals=0),
        name="open_second",
    )(where, query_second[0, 0], key_second[0, 0], value_second[0, 0])
    qkv = swap(qkv, "ylo")
    up = call(
        pack_body, sds((FOUR, tokens, cols), BF16), (where, up_raw), micros=1.4, name="pack"
    )
    qkv, up, other = lax.optimization_barrier((qkv, up, other))
    qkv = qkv.reshape(n, cols + 2 * HD)
    kvs = [lax.ppermute(qkv[:, cols:], SEQ, pairs) for pairs in (near, far, cross)]
    up = swap(up, "ylo").reshape(n, cols)
    kv_first = lax.all_gather(
        jnp.concatenate([kv1, other], axis=0), ROW, axis=0, tiled=True
    )

    long = pltpu.VMEM((length, HD), BF16)
    turned = pltpu.VMEM((HD, length), BF16)
    bias = pltpu.VMEM((length, n), F32)
    total = pltpu.VMEM((length, HD), F32)

    out2, lse, stats = call(
        functools.partial(forward_body, heads),
        (sds((n, cols), BF16), sds((heads, n), F32), sds((FOUR, 8, n), F32)),
        (where, qkv, *kvs, up, gain_cols),
        [long, long, bias],
        micros=6.4,
        name="forward_second",
    )
    stats = swap(stats, "ylo")
    dq, dkv = call(
        functools.partial(backward_body, heads, width),
        (
            sds((n, cols), BF16),
            sds((places, tokens + 16, 2 * HD), BF16),
        ),
        (where, qkv, *kvs, up, gain_cols, out2, lse, stats),
        [long, long, bias, total, total],
        micros=7.0,
        name="backward",
    )
    dkv = swap(dkv, SEQ)

    normed = call(
        first_body,
        sds((tokens, width), BF16),
        (where, query_first[0, 0], kv_first, gain),
        [
            long,
            turned,
            pltpu.VMEM((n, HD), BF16),
            pltpu.VMEM((tokens, width), BF16),
            bias,
        ],
        micros=7.0,
        name="forward_first",
    )
    next_input = along(normed, "pipe", 1, pipes)
    dq, dkv, normed = lax.optimization_barrier((dq, dkv, normed))
    dq = swap(dq.reshape(FOUR, tokens, cols), "ylo")
    grad_key, grad_value, share = call(
        gather_body,
        (sds((tokens, kv_width), BF16),) * 2 + (sds((1, 2 * HD), F32),),
        (where, dkv),
        name="gather",
    )
    grad_gain = lax.psum(share, "dp")
    grad_query = call(join_body, sds((tokens, width), BF16), (where, dq), name="join")
    return (
        next_input[None, None],
        grad_query[None, None],
        grad_key[None, None],
        grad_value[None, None],
        grad_gain,
    )


def solution(mesh):
    shape = mesh.devices.shape
    fine = Mesh(
        mesh.devices.reshape(shape[0], shape[1], 2, 2, shape[2] // 4),
        ("dp", "pipe", "zhi", "yhi", "ylo"),
    )
    big = P("dp", "pipe", SEQ, None)
    return jax.shard_map(
        local,
        mesh=fine,
        in_specs=(big,) * 7 + (P("pipe", None),),
        out_specs=(big,) * 4 + (P("pipe", SEQ),),
        check_vma=False,
    )
```

```python
import functools
import math

import jax
import jax.numpy as jnp
from jax import lax
from jax.experimental import pallas as pl
from jax.experimental.pallas import tpu as pltpu
from jax.sharding import Mesh
from jax.sharding import PartitionSpec as P

HD = 128
EPSILON = 1e-05
SCALE = 1.0 / math.sqrt(HD)
BINARY = SCALE / math.log(2.0)
F32 = jnp.float32
BF16 = jnp.bfloat16

ROW = ("yhi", "ylo")
SEQ = ("zhi", "yhi", "ylo")
FOUR = 4

VMEM = pl.BlockSpec(memory_space=pltpu.VMEM)
SMEM = pl.BlockSpec(memory_space=pltpu.SMEM)


def call(body, outs, inputs, scratch=(), micros=1.0, name=None):
    return pl.pallas_call(
        body,
        out_shape=outs,
        in_specs=[SMEM] + [VMEM] * (len(inputs) - 1),
        out_specs=jax.tree.map(lambda _: VMEM, outs),
        scratch_shapes=list(scratch),
        compiler_params=pltpu.CompilerParams(vmem_limit_bytes=48 * 1024 * 1024),
        cost_estimate=pl.CostEstimate(
            flops=int(micros * 1e9), bytes_accessed=0, transcendentals=0
        ),
        name=name,
    )(*inputs)


def sds(shape, dtype):
    return jax.ShapeDtypeStruct(shape, dtype)


def dot_nt(a, b):
    return lax.dot_general(a, b, (((1,), (1,)), ((), ())), preferred_element_type=F32)


def dot_nn(a, b):
    return lax.dot_general(a, b, (((1,), (0,)), ((), ())), preferred_element_type=F32)


def column(row):
    return jnp.broadcast_to(row, (HD, row.shape[1])).T


def row_of(block):
    return jnp.sum(block.T, axis=0, keepdims=True)


def head_at(where, place):
    return place + where[4] * (FOUR - 1 - 2 * place)


def head_columns(where, place, width):
    return pl.ds(pl.multiple_of(head_at(where, place) * width, width), width)


def attend(scores, values_t, bias):
    scores = scores + bias[...]
    highest = jnp.max(scores, axis=0, keepdims=True)
    exponent = jnp.exp2((scores - highest) * BINARY)
    total = jnp.sum(exponent, axis=0, keepdims=True)
    out = dot_nn(values_t, exponent.astype(BF16)) * (1.0 / total)
    return out.T.astype(BF16), highest * BINARY + jnp.log2(total)


def ahead_of(count, make):
    after = make(0)
    for i in range(count):
        now = after
        if i + 1 < count:
            after = make(i + 1)
        yield i, now


def set_bias(where, bias):
    shape = bias.shape
    ahead = lax.broadcasted_iota(jnp.int32, shape, 0) - lax.broadcasted_iota(jnp.int32, shape, 1)
    bias[...] = jnp.where(ahead <= where[0] * shape[1], 0.0, -jnp.inf).astype(F32)


def load_keys(where, blocks, at, full):
    n = blocks[0].shape[0]
    for i, block in enumerate(blocks):
        group = where[0] if i == 0 else where[4 + i]
        full[pl.ds(pl.multiple_of(group * n, n), n), :] = block[:, at : at + HD]


def open_body(where, query, keys, values, out):
    width = query.shape[1] // FOUR
    for place in range(FOUR):
        cols = head_columns(where, place, HD)
        out[place, :, :width] = query[:, head_columns(where, place, width)]
        out[place, :, width : width + HD] = keys[:, cols]
        out[place, :, width + HD :] = values[:, cols]


def pack_body(where, full, out):
    for place in range(FOUR):
        out[place] = full[:, head_columns(where, place, out.shape[2])]


def join_body(where, parts, out):
    for place in range(FOUR):
        out[:, head_columns(where, place, parts.shape[2])] = parts[place]


def gather_body(where, parts, keys, values, share):
    tokens = keys.shape[0]
    for h in range(FOUR):
        cols = slice(h * HD, (h + 1) * HD)
        total = 0.0
        for group in range(parts.shape[0] // FOUR):
            place = FOUR - 1 - h if group % 2 else h
            total = total + parts[group * FOUR + place, :tokens].astype(F32)
        keys[:, cols] = total[:, :HD].astype(BF16)
        values[:, cols] = total[:, HD:].astype(BF16)
    terms = parts[0, tokens:].astype(F32)
    for s in range(1, parts.shape[0]):
        terms = terms + parts[s, tokens:].astype(F32)
    share[...] = terms[0:1] + terms[1:2] + terms[2:3]


def forward_body(heads, where, q, kv1, kv2, kv3, up, gain, out, lse, stats, k_s, v_s, bias):
    set_bias(where, bias)
    blocks = (q.at[:, heads * HD :], kv1, kv2, kv3)
    load_keys(where, blocks, 0, k_s)
    load_keys(where, blocks, HD, v_s)
    values_t = v_s[...].T
    n = bias.shape[1]
    square = jnp.zeros((n, HD), F32)
    cross = jnp.zeros((n, HD), F32)
    for h, scores in ahead_of(heads, lambda h: dot_nt(k_s[...], q[:, h * HD : (h + 1) * HD])):
        cols = slice(h * HD, (h + 1) * HD)
        result, lse[h : h + 1, :] = attend(scores, values_t, bias)
        out[:, cols] = result
        value = result.astype(F32)
        square = square + value * value
        cross = cross + gain[:, cols].astype(F32) * up[:, cols].astype(F32) * value
    rows = jnp.concatenate(
        [row_of(square), row_of(cross), jnp.zeros((stats.shape[1] - 2, n), F32)], axis=0
    )
    for place in range(FOUR):
        stats[place] = rows


def backward_body(
    heads, width, where, q, kv1, kv2, kv3, up, gain, act, lse, stats,
    dq, dkv, k_s, v_s, bias, dk_s, dv_s,
):
    set_bias(where, bias)
    blocks = (q.at[:, heads * HD :], kv1, kv2, kv3)
    load_keys(where, blocks, 0, k_s)
    load_keys(where, blocks, HD, v_s)
    keys_t = k_s[...].T
    totals = (stats[0] + stats[1]) + (stats[2] + stats[3])
    inverse_row = lax.rsqrt(totals[0:1] / width + EPSILON)
    inverse = column(inverse_row)
    shrink = column(inverse_row * inverse_row * inverse_row * (totals[1:2] / width))
    sums = []
    for h in range(heads):
        cols = slice(h * HD, (h + 1) * HD)
        queries = q[:, cols]
        act_h = act[:, cols].astype(F32)
        upstream = up[:, cols].astype(F32)
        sums.append(jnp.sum(upstream * act_h * inverse, axis=0, keepdims=True))
        grad = (gain[:, cols].astype(F32) * upstream * inverse - act_h * shrink).astype(BF16)
        dots = row_of(grad.astype(F32) * act_h)
        scores = dot_nt(k_s[...], queries) * BINARY + bias[...]
        probs = jnp.exp2(scores - lse[h : h + 1, :])
        grad_weights = dot_nt(v_s[...], grad)
        grad_scores = (probs * (grad_weights - dots) * SCALE).astype(BF16)
        dv = dot_nn(probs.astype(BF16), grad)
        dk = dot_nn(grad_scores, queries)
        if h == 0:
            dv_s[...] = dv
            dk_s[...] = dk
        else:
            dv_s[...] += dv
            dk_s[...] += dk
        dq[:, cols] = dot_nn(keys_t, grad_scores).T.astype(BF16)
    tokens = dk_s.shape[0] // dkv.shape[0]
    per = heads // FOUR
    extra = dkv.shape[1] - tokens
    for s in range(dkv.shape[0]):
        rows = slice(s * tokens, (s + 1) * tokens)
        dkv[s, :tokens, :HD] = dk_s[rows].astype(BF16)
        dkv[s, :tokens, HD:] = dv_s[rows].astype(BF16)
        j = s % FOUR
        value = jnp.concatenate(sums[j * per : (j + 1) * per], axis=1)
        value = jnp.where(where[2] == s // FOUR, value, 0.0)
        terms = []
        for _ in range(3):
            term = value.astype(BF16).astype(F32)
            terms.append(term)
            value = value - term
        terms.append(jnp.zeros((extra - 3, value.shape[1]), F32))
        dkv[s, tokens:] = jnp.concatenate(terms, axis=0).astype(BF16)


def first_body(where, q, kv, gain, out, k_s, vt_s, q_s, o_s, bias):
    tokens, width = q.shape
    length = kv.shape[0]
    kv_heads = kv.shape[1] // (2 * HD)
    heads = width // HD
    n = bias.shape[1]
    together = n // tokens
    ids = lax.broadcasted_iota(jnp.int32, (length, n), 0)
    query_ids = lax.broadcasted_iota(jnp.int32, (length, n), 1) % tokens
    block = ids // tokens
    half = (block % 2 + where[1]) % 2
    key_at = half * (length // 2) + (block // 2) * tokens + ids % tokens
    query_at = where[1] * (length // 2) + where[3] * tokens + query_ids
    bias[...] = jnp.where(key_at <= query_at, 0.0, -jnp.inf).astype(F32)
    square = jnp.zeros((tokens, HD), F32)
    for g in range(kv_heads):
        k_s[...] = kv[:, g * HD : (g + 1) * HD]
        vt_s[...] = kv[:, (kv_heads + g) * HD : (kv_heads + g + 1) * HD].T
        for part in range(heads // kv_heads // together):
            start = g * (heads // kv_heads) + part * together
            for i in range(together):
                q_s[i * tokens : (i + 1) * tokens, :] = q[:, (start + i) * HD : (start + i + 1) * HD]
            result, _ = attend(dot_nt(k_s[...], q_s[...]), vt_s[...], bias)
            for i in range(together):
                piece = result[i * tokens : (i + 1) * tokens]
                o_s[:, (start + i) * HD : (start + i + 1) * HD] = piece
                piece = piece.astype(F32)
                square = square + piece * piece
    mean = jnp.sum(square, axis=1, keepdims=True) / width
    inverse = jnp.broadcast_to(lax.rsqrt(mean + EPSILON), (tokens, HD))
    for h in range(heads):
        cols = slice(h * HD, (h + 1) * HD)
        out[:, cols] = (gain[:, cols].astype(F32) * o_s[:, cols].astype(F32) * inverse).astype(BF16)


def local(
    query_first, key_first, value_first, query_second, key_second, value_second, grad_output, gain
):
    tokens, width = query_first.shape[2:]
    kv_width = key_first.shape[3]
    n = tokens * FOUR
    cols = width // FOUR
    heads = cols // HD
    places = lax.axis_size(SEQ)
    length = tokens * places
    pipes = lax.axis_size("pipe")
    zhi, yhi, ylo = (lax.axis_index(axis) for axis in SEQ)
    group = zhi * 2 + yhi
    mine = ylo + yhi * (FOUR - 1 - 2 * ylo)
    where = jnp.stack(
        [group, zhi, mine, yhi * FOUR + ylo, yhi, 3 - group, 2 - zhi * 2 + yhi, zhi * 2 + 1 - yhi]
    ).astype(jnp.int32)
    gain_cols = lax.dynamic_slice_in_dim(gain, mine * cols, cols, 1)

    def device(z, h, y):
        return (z * 2 + h) * FOUR + y

    near = [(device(z, 0, y), device(z, 1, 3 - y)) for z in range(2) for y in range(FOUR)]
    far = [(device(0, h, y), device(1, h, y)) for h in range(2) for y in range(FOUR)]
    cross = [(device(0, h, y), device(1, 1 - h, 3 - y)) for h in range(2) for y in range(FOUR)]

    def swap(packed, axes):
        return lax.all_to_all(packed, axes, split_axis=0, concat_axis=0, tiled=True)

    def along(value, axis, step, count):
        return lax.ppermute(value, axis, [(i, (i + step) % count) for i in range(count)])

    up_raw = along(grad_output[0, 0], "pipe", -1, pipes)
    kv1 = jnp.concatenate([key_first[0, 0], value_first[0, 0]], axis=1)
    other = lax.ppermute(kv1, "zhi", [(0, 1)])
    qkv = pl.pallas_call(
        open_body,
        grid=(1,),
        in_specs=[
            SMEM,
            pl.BlockSpec((tokens, width), lambda i: (0, 0)),
            pl.BlockSpec((tokens, kv_width), lambda i: (0, 0)),
            pl.BlockSpec((tokens, kv_width), lambda i: (0, 0)),
        ],
        out_specs=pl.BlockSpec((FOUR, tokens, cols + 2 * HD), lambda i: (0, 0, 0)),
        out_shape=sds((FOUR, tokens, cols + 2 * HD), BF16),
        cost_estimate=pl.CostEstimate(flops=10**9, bytes_accessed=0, transcendentals=0),
        name="open_second",
    )(where, query_second[0, 0], key_second[0, 0], value_second[0, 0])
    qkv = swap(qkv, "ylo")
    up = call(
        pack_body, sds((FOUR, tokens, cols), BF16), (where, up_raw), micros=1.4, name="pack"
    )
    qkv, up, other = lax.optimization_barrier((qkv, up, other))
    qkv = qkv.reshape(n, cols + 2 * HD)
    kvs = [lax.ppermute(qkv[:, cols:], SEQ, pairs) for pairs in (cross, far, near)]
    up = swap(up, "ylo").reshape(n, cols)
    kv_first = lax.all_gather(
        jnp.concatenate([kv1, other], axis=0), ROW, axis=0, tiled=True
    )

    long = pltpu.VMEM((length, HD), BF16)
    turned = pltpu.VMEM((HD, length), BF16)
    bias = pltpu.VMEM((length, n), F32)
    total = pltpu.VMEM((length, HD), F32)

    out2, lse, stats = call(
        functools.partial(forward_body, heads),
        (sds((n, cols), BF16), sds((heads, n), F32), sds((FOUR, 8, n), F32)),
        (where, qkv, *kvs, up, gain_cols),
        [long, long, bias],
        micros=6.4,
        name="forward_second",
    )
    stats = swap(stats, "ylo")
    dq, dkv = call(
        functools.partial(backward_body, heads, width),
        (
            sds((n, cols), BF16),
            sds((places, tokens + 16, 2 * HD), BF16),
        ),
        (where, qkv, *kvs, up, gain_cols, out2, lse, stats),
        [long, long, bias, total, total],
        micros=7.0,
        name="backward",
    )
    dkv = swap(dkv, SEQ)

    normed = call(
        first_body,
        sds((tokens, width), BF16),
        (where, query_first[0, 0], kv_first, gain),
        [
            long,
            turned,
            pltpu.VMEM((n, HD), BF16),
            pltpu.VMEM((tokens, width), BF16),
            bias,
        ],
        micros=7.0,
        name="forward_first",
    )
    next_input = along(normed, "pipe", 1, pipes)
    dq, dkv, normed = lax.optimization_barrier((dq, dkv, normed))
    dq = swap(dq.reshape(FOUR, tokens, cols), "ylo")
    grad_key, grad_value, share = call(
        gather_body,
        (sds((tokens, kv_width), BF16),) * 2 + (sds((1, 2 * HD), F32),),
        (where, dkv),
        name="gather",
    )
    grad_gain = lax.psum(share, "dp")
    grad_query = call(join_body, sds((tokens, width), BF16), (where, dq), name="join")
    return (
        next_input[None, None],
        grad_query[None, None],
        grad_key[None, None],
        grad_value[None, None],
        grad_gain,
    )


def solution(mesh):
    shape = mesh.devices.shape
    fine = Mesh(
        mesh.devices.reshape(shape[0], shape[1], 2, 2, shape[2] // 4),
        ("dp", "pipe", "zhi", "yhi", "ylo"),
    )
    big = P("dp", "pipe", SEQ, None)
    return jax.shard_map(
        local,
        mesh=fine,
        in_specs=(big,) * 7 + (P("pipe", None),),
        out_specs=(big,) * 4 + (P("pipe", SEQ),),
        check_vma=False,
    )
```
